512 devices in a mesh: lon: 128 (over x_lo, z, y), lat: 4 (over x_hi, core).
Axes of the slice: x: 4 (x_hi: 2, x_lo: 2; x = x_hi * 2 + x_lo), y: 8, z: 8, core: 2. Of those that a mesh axis runs over, the one named last changes fastest.
Arguments:
- features: bfloat16 [320, 2048, 384], P('lat', 'lon'), may hold values from -6 to 6
- filter_basis: bfloat16 [3, 5, 17, 320], replicated, may hold values from -0.8984375 to 0.8984375
- half_widths: int32 [320], replicated, may hold values from 1 to 8, as said below
- mixing: bfloat16 [1152, 384], replicated, may hold values from -0.1875 to 0.1875
- channel_bias: float32 [384], replicated, may hold values from -3 to 3
- cotangent: bfloat16 [320, 2048, 384], P('lat', 'lon'), may hold values from -6 to 6
Outputs:
- input_grad: bfloat16 [320, 2048, 384], P('lat', 'lon')
- mixing_grad: bfloat16 [1152, 384], replicated
The draws below stay inside these ranges and needn't reach their ends.
Inputs may be any that keep to these rules, and one draw needn't show every extreme that they name: `half_widths`: the first and last latitude rows have exactly 8.
All inputs are finite; a program needn't handle non-finite values.
Results may differ from the reference program's by a relative error of at most 0.0063.
Values may be sent and summed in bfloat16 or wider, within the bound.
A program may use at most 128 MiB of HBM per device.

```python
import math
import jax
import jax.numpy as jnp
from jax import lax

CHANNELS = 384
KERNELS = 3
REACH = 2
HALO = 8
LAT = 320
LON = 2048
TAPS_LAT = 5
TAPS_LON = 17


def draw_half_widths(key, part):
    key = jax.random.fold_in(key, 11)
    rows = jnp.arange(LAT, dtype=jnp.int32)
    distance = jnp.abs(2 * rows - (LAT - 1))
    base_width = 1 + distance * (HALO - 1) // (LAT - 1)
    jitter = jax.random.randint(key, (LAT,), -1, 2, dtype=jnp.int32)
    widths = jnp.clip(base_width + jitter, 1, HALO)
    polar = (rows == 0) | (rows == LAT - 1)
    return jnp.where(polar, HALO, widths).astype(jnp.int32)


def block_levels(rng, shape, pieces, smallest, largest):
    level, own = 1.0, jax.random.fold_in(rng, 6)
    for dim, shards_of in pieces:
        draws = jnp.exp(jax.random.uniform(jax.random.fold_in(own, dim), (shards_of,), jnp.float32, smallest / len(pieces), largest / len(pieces)))
        level = level * jnp.repeat(draws, shape[dim] // shards_of).reshape([-1 if axis == dim else 1 for axis in range(len(shape))])
    return level


def normal_values(rng, shape, width, reach, cuts=(), kind=jnp.bfloat16):
    level = block_levels(rng, shape, cuts, -0.22, 0.18) if cuts else 1.0
    drawn = jax.random.normal(rng, shape, jnp.float32) * width * level
    return jnp.minimum(jnp.maximum(drawn, -reach), reach).astype(kind)


def setup_inputs(seed: int = 0) -> dict:
    seeds = jax.random.split(jax.random.key(seed), 7)
    return {
        "features": normal_values(seeds[0], (LAT, LON, CHANNELS), 1.0, 6.0, ((0, 4), (1, 128))),
        "filter_basis": normal_values(seeds[1], (KERNELS, TAPS_LAT, TAPS_LON, LAT), 0.15, 0.8984375),
        "half_widths": draw_half_widths(jax.random.fold_in(seeds[6], 71), 0),
        "mixing": normal_values(seeds[3], (KERNELS * CHANNELS, CHANNELS), (KERNELS * CHANNELS) ** -0.5, 0.1875),
        "channel_bias": normal_values(seeds[4], (CHANNELS,), 0.5, 3.0, (), jnp.float32),
        "cotangent": normal_values(seeds[5], (LAT, LON, CHANNELS), 1.0, 6.0, ((0, 4), (1, 128))),
    }


def gelu_exact(values):
    return jax.nn.gelu(values, approximate=False)

def reference(features, filter_basis, half_widths, mixing, channel_bias, cotangent):
    taps_lat = 2 * REACH + 1
    taps_lon = 2 * HALO + 1
    offsets = jnp.abs(jnp.arange(taps_lon, dtype=jnp.int32) - HALO)
    allowed = (offsets[:, None] <= half_widths[None, :]).astype(jnp.float32)
    masked = filter_basis.astype(jnp.float32) * allowed[None, None]
    masked_pad = jnp.pad(masked, ((0, 0), (0, 0), (0, 0), (REACH, REACH)))
    feature_pad = jnp.pad(features, ((REACH, REACH), (0, 0), (0, 0)))

    def forward_row(carry, row):
        rows = lax.dynamic_slice_in_dim(feature_pad, row, taps_lat, 0).astype(jnp.float32)
        coeffs = lax.dynamic_slice_in_dim(masked, row, 1, 3)[:, :, :, 0]
        filtered = jnp.zeros((LON, KERNELS, CHANNELS), jnp.float32)
        for tap in range(taps_lon):
            moved = jnp.roll(rows, HALO - tap, axis=1)
            filtered = filtered + jnp.einsum('bs,sjc->jbc', coeffs[:, :, tap], moved)
        flat = filtered.astype(jnp.bfloat16).reshape(LON, KERNELS * CHANNELS)
        pre = jnp.dot(flat, mixing, preferred_element_type=jnp.float32) + channel_bias
        _, pullback = jax.vjp(gelu_exact, pre)
        grad_pre, = pullback(cotangent[row].astype(jnp.float32))
        grad_pre = grad_pre.astype(jnp.bfloat16)
        carry = carry + lax.dot_general(flat, grad_pre, (((0,), (0,)), ((), ())), preferred_element_type=jnp.float32)
        return (carry, grad_pre)
    start_sum = jnp.zeros((KERNELS * CHANNELS, CHANNELS), jnp.float32)
    total, grad_rows = lax.scan(forward_row, start_sum, jnp.arange(LAT, dtype=jnp.int32))
    mixing_grad = (total / math.sqrt(LAT * LON)).astype(jnp.bfloat16)
    grad_pad = jnp.pad(grad_rows, ((REACH, REACH), (0, 0), (0, 0)))
    transposed = mixing.reshape(KERNELS, CHANNELS, CHANNELS).transpose(0, 2, 1).reshape(KERNELS * CHANNELS, CHANNELS)

    def backward_row(row):
        rows = lax.dynamic_slice_in_dim(grad_pad, row, taps_lat, 0).astype(jnp.float32)
        coeffs = lax.dynamic_slice_in_dim(masked_pad, row, taps_lat, 3)
        chosen = jnp.stack([coeffs[:, offset, :, taps_lat - 1 - offset] for offset in range(taps_lat)], axis=1)
        ordered = rows[::-1]
        spread = jnp.zeros((LON, KERNELS, CHANNELS), jnp.float32)
        for tap in range(taps_lon):
            moved = jnp.roll(ordered, tap - HALO, axis=1)
            spread = spread + jnp.einsum('bs,sjc->jbc', chosen[:, :, tap], moved)
        flat = spread.astype(jnp.bfloat16).reshape(LON, KERNELS * CHANNELS)
        branch = jnp.dot(flat, transposed, preferred_element_type=jnp.float32)
        return (cotangent[row].astype(jnp.float32) + branch).astype(jnp.bfloat16)
    input_grad = lax.map(backward_row, jnp.arange(LAT, dtype=jnp.int32))
    return (input_grad, mixing_grad)
```

```python
import math

import jax
import jax.numpy as jnp
from jax import lax
from jax.experimental import pallas as pl
from jax.experimental.pallas import tpu as pltpu
from jax.sharding import PartitionSpec as P

MESH = pl.DeviceIdType.MESH
SIZE_X_LO, SIZE_Z, SIZE_Y = 2, 8, 8
SIZE_X = 4


def position():
    lon, lat = lax.axis_index("lon"), lax.axis_index("lat")
    x = lax.div(lat, 2) * SIZE_X_LO + lax.div(lon, SIZE_Z * SIZE_Y)
    z = lax.rem(lax.div(lon, SIZE_Y), SIZE_Z)
    return x, z, lax.rem(lon, SIZE_Y), lax.rem(lat, 2)


def device(x, z, y, core):
    lon = (lax.rem(x, SIZE_X_LO) * SIZE_Z + z) * SIZE_Y + y
    return {"lon": lon, "lat": lax.div(x, SIZE_X_LO) * 2 + core}


def sum_peers():
    x, z, y, core = position()
    peers = [device(x, z, y, 1 - core)]
    peers += [device(lax.rem(x + d, SIZE_X), z, y, core) for d in range(1, SIZE_X)]
    peers += [device(x, lax.rem(z + d, SIZE_Z), y, core) for d in range(1, SIZE_Z)]
    peers += [device(x, z, lax.rem(y + d, SIZE_Y), core) for d in range(1, SIZE_Y)]
    return peers


def greet(peers):
    barrier = pltpu.get_barrier_semaphore()
    for peer in peers:
        pl.semaphore_signal(barrier, inc=1, device_id=peer, device_id_type=MESH)
    pl.semaphore_wait(barrier, len(peers))


def sum_buffers(part_rows, channels):
    tiles = (part_rows // 16) * (channels // 128)
    share = -(-tiles // SIZE_Z)
    copies = 2 + 2 * (SIZE_X - 1) + 2 * (SIZE_Z - 1) + SIZE_Y - 1
    return [
        pltpu.VMEM((SIZE_X, part_rows, channels), jnp.float32),
        pltpu.VMEM((SIZE_X, part_rows, channels), jnp.bfloat16),
        pltpu.VMEM((SIZE_X - 1, part_rows, channels), jnp.bfloat16),
        pltpu.VMEM((SIZE_Z, share, 16, 128), jnp.float32),
        pltpu.VMEM((SIZE_Z, share, 16, 128), jnp.bfloat16),
        pltpu.VMEM((SIZE_Z - 1, share, 16, 128), jnp.bfloat16),
        pltpu.VMEM((SIZE_Y, share, 16, 128), jnp.bfloat16),
        pltpu.VMEM((SIZE_Z, share, 16, 128), jnp.bfloat16),
        pltpu.VMEM((2, SIZE_X, part_rows, channels), jnp.bfloat16),
        pltpu.SemaphoreType.DMA((copies,)),
        pltpu.SemaphoreType.DMA((copies,)),
    ]


class SumOverAll:
    def __init__(self, local, buffers, scale):
        self.local, self.scale = local, scale
        (self.half, self.x_out, self.x_in, self.z_own, self.z_out, self.z_in, self.y_all, self.z_done, self.done,
         self.send, self.recv) = buffers
        self.x, self.z, self.y, self.core = position()
        self.used = 0
        self.rows, self.channels = local.shape[2:]
        self.lanes = self.channels // 128
        self.tiles = (self.rows // 16) * self.lanes
        self.share = self.z_own.shape[1]

    def copy(self, src, dst, peer):
        index = self.used
        self.used += 1
        copy = pltpu.make_async_remote_copy(
            src_ref=src, dst_ref=dst, send_sem=self.send.at[index], recv_sem=self.recv.at[index],
            device_id=peer, device_id_type=MESH)
        copy.start()
        return copy

    def tile(self, t):
        row, lane = t // self.lanes * 16, t % self.lanes * 128
        return slice(row, row + 16), slice(lane, lane + 128)

    def start_core(self):
        self.flying = [self.copy(self.local.at[1 - self.core], self.half, device(self.x, self.z, self.y, 1 - self.core))]

    def wait(self):
        for copy in self.flying:
            copy.wait()

    def finish_core_start_x(self):
        self.wait()
        for part in range(SIZE_X):
            total = self.half[part] + self.local[self.core, part]
            self.half[part] = total
            self.x_out[part] = total.astype(jnp.bfloat16)
        self.flying = []
        for d in range(1, SIZE_X):
            peer = lax.rem(self.x + d, SIZE_X)
            self.flying.append(self.copy(self.x_out.at[peer], self.x_in.at[d - 1], device(peer, self.z, self.y, self.core)))

    def finish_x_start_z(self):
        self.wait()
        for t in range(SIZE_Z * self.share):
            group, slot = t // self.share, t % self.share
            if t < self.tiles:
                rows, lanes = self.tile(t)
                total = self.half[self.x, rows, lanes]
                for d in range(1, SIZE_X):
                    total = total + self.x_in[d - 1, rows, lanes].astype(jnp.float32)
            else:
                total = jnp.zeros((16, 128), jnp.float32)
            self.z_own[group, slot] = total
            self.z_out[group, slot] = total.astype(jnp.bfloat16)
        self.flying = []
        for d in range(1, SIZE_Z):
            peer = lax.rem(self.z + d, SIZE_Z)
            self.flying.append(self.copy(self.z_out.at[peer], self.z_in.at[d - 1], device(self.x, peer, self.y, self.core)))

    def finish_z_start_y(self):
        self.wait()
        total = self.z_own[self.z]
        for d in range(1, SIZE_Z):
            total = total + self.z_in[d - 1].astype(jnp.float32)
        self.y_all[self.y] = total.astype(jnp.bfloat16)
        self.flying = []
        for d in range(1, SIZE_Y):
            peer = lax.rem(self.y + d, SIZE_Y)
            self.flying.append(self.copy(self.y_all.at[self.y], self.y_all.at[self.y], device(self.x, self.z, peer, self.core)))

    def finish_y_start_gather(self):
        self.wait()
        total = self.y_all[0].astype(jnp.float32)
        for other in range(1, SIZE_Y):
            total = total + self.y_all[other].astype(jnp.float32)
        self.z_done[self.z] = (total / self.scale).astype(jnp.bfloat16)
        self.flying = []
        for d in range(1, SIZE_Z):
            peer = lax.rem(self.z + d, SIZE_Z)
            self.flying.append(self.copy(self.z_done.at[self.z], self.z_done.at[self.z], device(self.x, peer, self.y, self.core)))

    def finish_z_gather_x(self):
        self.wait()
        for t in range(self.tiles):
            rows, lanes = self.tile(t)
            self.done[self.core, self.x, rows, lanes] = self.z_done[t // self.share, t % self.share]
        self.flying = []
        block = self.done.at[self.core, self.x]
        for d in range(1, SIZE_X):
            peer = lax.rem(self.x + d, SIZE_X)
            self.flying.append(self.copy(block, block, device(peer, self.z, self.y, self.core)))

    def finish_x_gather_core(self):
        self.wait()
        block = self.done.at[self.core]
        self.flying = [self.copy(block, block, device(self.x, self.z, self.y, 1 - self.core))]

    def finish(self, out):
        self.wait()
        for core in range(2):
            for part in range(SIZE_X):
                at = (core * SIZE_X + part) * self.rows
                out[at : at + self.rows, :] = self.done[core, part]


def sum_kernel(scale, local, out, *buffers):
    greet(sum_peers())
    work = SumOverAll(local, buffers, scale)
    work.start_core()
    work.finish_core_start_x()
    work.finish_x_start_z()
    work.finish_z_start_y()
    work.finish_y_start_gather()
    work.finish_z_gather_x()
    work.finish_x_gather_core()
    work.finish(out)


def sum_over_all(local, scale):
    rows, channels = local.shape
    part_rows = rows // (2 * SIZE_X)
    return pl.pallas_call(
        lambda *refs: sum_kernel(scale, *refs),
        out_shape=jax.ShapeDtypeStruct((rows, channels), jnp.bfloat16),
        in_specs=[pl.BlockSpec(memory_space=pltpu.VMEM)],
        out_specs=pl.BlockSpec(memory_space=pltpu.VMEM),
        scratch_shapes=sum_buffers(part_rows, channels),
        compiler_params=pltpu.CompilerParams(
            collective_id=0, has_side_effects=True, vmem_limit_bytes=32 * 1024 * 1024),
    )(local.reshape(2, SIZE_X, part_rows, channels))


def extended_2(block, sides, width, periodic):
    for axis, dim in sides:
        count = lax.axis_size(axis)
        forward = [(i, i + 1) for i in range(count - 1)]
        if periodic:
            forward.append((count - 1, 0))
        backward = [(target, source) for source, target in forward]
        low = lax.ppermute(
            lax.slice_in_dim(block, block.shape[dim] - width, None, axis=dim), axis, forward
        )
        high = lax.ppermute(lax.slice_in_dim(block, 0, width, axis=dim), axis, backward)
        block = jnp.concatenate([low, block, high], axis=dim)
    return block


def gelu_exact(values):
    return jax.nn.gelu(values, approximate=False)


def basis_window(filter_basis, half_widths, row_start, rows_here, reach, halo):
    taps_lon = 2 * halo + 1
    offsets = jnp.abs(jnp.arange(taps_lon, dtype=jnp.int32) - halo)
    allowed = (offsets[:, None] <= half_widths[None, :]).astype(jnp.float32)
    masked = filter_basis.astype(jnp.float32) * allowed[None, None]
    padded = jnp.pad(masked, ((0, 0), (0, 0), (0, 0), (reach, reach)))
    return lax.dynamic_slice_in_dim(padded, row_start, rows_here + 2 * reach, 3)


def band_matrix(rows_taps, shift_table):
    band = jnp.einsum("bsqa,qvu->avbsu", rows_taps, shift_table, precision=lax.Precision.HIGHEST)
    count_rows, width_out, kernels, taps_lat, width_in = band.shape
    return band.reshape(count_rows, width_out * kernels, taps_lat * width_in).astype(jnp.bfloat16)


def stacked_rows(extended, rows_here, taps_lat):
    pieces = [extended[offset : offset + rows_here] for offset in range(taps_lat)]
    stacked = jnp.stack(pieces, axis=1)
    return stacked.reshape(rows_here, -1, stacked.shape[-1])


def contract(band, windows):
    return jnp.einsum("anm,amc->anc", band, windows, preferred_element_type=jnp.float32)


def extend_lat(block, reach):
    return extended_2(block, (("lat", 0),), reach, False)


def apply_band(band, lat_ext, halo, rows_here, taps_lat):
    padded = extended_2(lat_ext, (("lon", 1),), halo, True)
    return contract(band, stacked_rows(padded, rows_here, taps_lat))


def per_device(features, filter_basis, half_widths, mixing, channel_bias, cotangent):
    rows_here, width_here, channels = features.shape
    kernels, taps_lat, taps_lon, total_rows = filter_basis.shape
    reach = (taps_lat - 1) // 2
    halo = (taps_lon - 1) // 2
    row_start = lax.axis_index("lat") * rows_here
    window = basis_window(filter_basis, half_widths, row_start, rows_here, reach, halo)
    span = width_here + 2 * halo
    tap_ids = jnp.arange(taps_lon, dtype=jnp.int32)[:, None, None]
    out_ids = jnp.arange(width_here, dtype=jnp.int32)[None, :, None]
    in_ids = jnp.arange(span, dtype=jnp.int32)[None, None, :]
    forward_table = (in_ids - out_ids == tap_ids).astype(jnp.float32)
    backward_table = (out_ids + 2 * halo - in_ids == tap_ids).astype(jnp.float32)
    forward_band = band_matrix(window[:, :, :, reach : reach + rows_here], forward_table)
    backward_rows = jnp.stack(
        [
            window[:, taps_lat - 1 - offset, :, offset : offset + rows_here]
            for offset in range(taps_lat)
        ],
        axis=1,
    )
    backward_band = band_matrix(backward_rows, backward_table)
    filtered = apply_band(forward_band, extend_lat(features, reach), halo, rows_here, taps_lat)
    flat = filtered.astype(jnp.bfloat16).reshape(rows_here * width_here, kernels * channels)
    pre = jnp.dot(flat, mixing, preferred_element_type=jnp.float32) + channel_bias
    cell_grads = cotangent.reshape(rows_here * width_here, channels).astype(jnp.float32)
    _, pullback = jax.vjp(gelu_exact, pre)
    (grad_pre,) = pullback(cell_grads)
    grad_pre = grad_pre.astype(jnp.bfloat16)
    local_sum = lax.dot_general(
        flat, grad_pre, (((0,), (0,)), ((), ())), preferred_element_type=jnp.float32
    )
    cell_count = rows_here * lax.axis_size("lat") * width_here * lax.axis_size("lon")
    mixing_grad = sum_over_all(local_sum, math.sqrt(cell_count))
    grad_grid = grad_pre.reshape(rows_here, width_here, channels)
    spread = apply_band(backward_band, extend_lat(grad_grid, reach), halo, rows_here, taps_lat)
    transposed = (
        mixing.reshape(kernels, channels, channels)
        .transpose(0, 2, 1)
        .reshape(kernels * channels, channels)
    )
    branch = jnp.dot(
        spread.astype(jnp.bfloat16).reshape(rows_here * width_here, kernels * channels),
        transposed,
        preferred_element_type=jnp.float32,
    )
    input_grad = (cell_grads + branch).astype(jnp.bfloat16).reshape(rows_here, width_here, channels)
    return (input_grad, mixing_grad)


def solution(mesh):
    return jax.shard_map(
        per_device,
        mesh=mesh,
        in_specs=(P("lat", "lon", None), P(), P(), P(), P(), P("lat", "lon", None)),
        out_specs=(P("lat", "lon", None), P()),
        check_vma=False,
    )
```

```python
import math

import jax
import jax.numpy as jnp
from jax import lax
from jax.experimental import pallas as pl
from jax.experimental.pallas import tpu as pltpu
from jax.sharding import PartitionSpec as P

MESH = pl.DeviceIdType.MESH
SIZE_X_LO, SIZE_Z, SIZE_Y = 2, 8, 8
SIZE_X = 4


def position():
    lon, lat = lax.axis_index("lon"), lax.axis_index("lat")
    x = lax.div(lat, 2) * SIZE_X_LO + lax.div(lon, SIZE_Z * SIZE_Y)
    z = lax.rem(lax.div(lon, SIZE_Y), SIZE_Z)
    return x, z, lax.rem(lon, SIZE_Y), lax.rem(lat, 2)


def device(x, z, y, core):
    lon = (lax.rem(x, SIZE_X_LO) * SIZE_Z + z) * SIZE_Y + y
    return {"lon": lon, "lat": lax.div(x, SIZE_X_LO) * 2 + core}


def sum_peers():
    x, z, y, core = position()
    peers = [device(x, z, y, 1 - core)]
    peers += [device(lax.rem(x + d, SIZE_X), z, y, core) for d in range(1, SIZE_X)]
    peers += [device(x, lax.rem(z + d, SIZE_Z), y, core) for d in range(1, SIZE_Z)]
    peers += [device(x, z, lax.rem(y + d, SIZE_Y), core) for d in range(1, SIZE_Y)]
    return peers


def greet(peers):
    barrier = pltpu.get_barrier_semaphore()
    for peer in peers:
        pl.semaphore_signal(barrier, inc=1, device_id=peer, device_id_type=MESH)
    pl.semaphore_wait(barrier, len(peers))


def sum_buffers(part_rows, channels):
    tiles = (part_rows // 16) * (channels // 128)
    share = -(-tiles // SIZE_Z)
    copies = 2 + 2 * (SIZE_X - 1) + 2 * (SIZE_Z - 1) + SIZE_Y - 1
    return [
        pltpu.VMEM((SIZE_X, part_rows, channels), jnp.float32),
        pltpu.VMEM((SIZE_X, part_rows, channels), jnp.bfloat16),
        pltpu.VMEM((SIZE_X - 1, part_rows, channels), jnp.bfloat16),
        pltpu.VMEM((SIZE_Z, share, 16, 128), jnp.float32),
        pltpu.VMEM((SIZE_Z, share, 16, 128), jnp.bfloat16),
        pltpu.VMEM((SIZE_Z - 1, share, 16, 128), jnp.bfloat16),
        pltpu.VMEM((SIZE_Y, share, 16, 128), jnp.bfloat16),
        pltpu.VMEM((SIZE_Z, share, 16, 128), jnp.bfloat16),
        pltpu.VMEM((2, SIZE_X, part_rows, channels), jnp.bfloat16),
        pltpu.SemaphoreType.DMA((copies,)),
        pltpu.SemaphoreType.DMA((copies,)),
    ]


class SumOverAll:
    def __init__(self, local, buffers, scale):
        self.local, self.scale = local, scale
        (self.half, self.x_out, self.x_in, self.z_own, self.z_out, self.z_in, self.y_all, self.z_done, self.done,
         self.send, self.recv) = buffers
        self.x, self.z, self.y, self.core = position()
        self.used = 0
        self.rows, self.channels = local.shape[2:]
        self.lanes = self.channels // 128
        self.tiles = (self.rows // 16) * self.lanes
        self.share = self.z_own.shape[1]

    def copy(self, src, dst, peer):
        index = self.used
        self.used += 1
        copy = pltpu.make_async_remote_copy(
            src_ref=src, dst_ref=dst, send_sem=self.send.at[index], recv_sem=self.recv.at[index],
            device_id=peer, device_id_type=MESH)
        copy.start()
        return copy

    def tile(self, t):
        row, lane = t // self.lanes * 16, t % self.lanes * 128
        return slice(row, row + 16), slice(lane, lane + 128)

    def start_core(self):
        self.flying = [self.copy(self.local.at[1 - self.core], self.half, device(self.x, self.z, self.y, 1 - self.core))]

    def wait(self):
        for copy in self.flying:
            copy.wait()

    def finish_core_start_x(self):
        self.wait()
        for part in range(SIZE_X):
            total = self.half[part] + self.local[self.core, part]
            self.half[part] = total
            self.x_out[part] = total.astype(jnp.bfloat16)
        self.flying = []
        for d in range(1, SIZE_X):
            peer = lax.rem(self.x + d, SIZE_X)
            self.flying.append(self.copy(self.x_out.at[peer], self.x_in.at[d - 1], device(peer, self.z, self.y, self.core)))

    def finish_x_start_z(self):
        self.wait()
        for t in range(SIZE_Z * self.share):
            group, slot = t // self.share, t % self.share
            if t < self.tiles:
                rows, lanes = self.tile(t)
                total = self.half[self.x, rows, lanes]
                for d in range(1, SIZE_X):
                    total = total + self.x_in[d - 1, rows, lanes].astype(jnp.float32)
            else:
                total = jnp.zeros((16, 128), jnp.float32)
            self.z_own[group, slot] = total
            self.z_out[group, slot] = total.astype(jnp.bfloat16)
        self.flying = []
        for d in range(1, SIZE_Z):
            peer = lax.rem(self.z + d, SIZE_Z)
            self.flying.append(self.copy(self.z_out.at[peer], self.z_in.at[d - 1], device(self.x, peer, self.y, self.core)))

    def finish_z_start_y(self):
        self.wait()
        total = self.z_own[self.z]
        for d in range(1, SIZE_Z):
            total = total + self.z_in[d - 1].astype(jnp.float32)
        self.y_all[self.y] = total.astype(jnp.bfloat16)
        self.flying = []
        for d in range(1, SIZE_Y):
            peer = lax.rem(self.y + d, SIZE_Y)
            self.flying.append(self.copy(self.y_all.at[self.y], self.y_all.at[self.y], device(self.x, self.z, peer, self.core)))

    def finish_y_start_gather(self):
        self.wait()
        total = self.y_all[0].astype(jnp.float32)
        for other in range(1, SIZE_Y):
            total = total + self.y_all[other].astype(jnp.float32)
        self.z_done[self.z] = (total / self.scale).astype(jnp.bfloat16)
        self.flying = []
        for d in range(1, SIZE_Z):
            peer = lax.rem(self.z + d, SIZE_Z)
            self.flying.append(self.copy(self.z_done.at[self.z], self.z_done.at[self.z], device(self.x, peer, self.y, self.core)))

    def finish_z_gather_x(self):
        self.wait()
        for t in range(self.tiles):
            rows, lanes = self.tile(t)
            self.done[self.core, self.x, rows, lanes] = self.z_done[t // self.share, t % self.share]
        self.flying = []
        block = self.done.at[self.core, self.x]
        for d in range(1, SIZE_X):
            peer = lax.rem(self.x + d, SIZE_X)
            self.flying.append(self.copy(block, block, device(peer, self.z, self.y, self.core)))

    def finish_x_gather_core(self):
        self.wait()
        block = self.done.at[self.core]
        self.flying = [self.copy(block, block, device(self.x, self.z, self.y, 1 - self.core))]

    def finish(self, out):
        self.wait()
        for core in range(2):
            for part in range(SIZE_X):
                at = (core * SIZE_X + part) * self.rows
                out[at : at + self.rows, :] = self.done[core, part]


def halo_peers():
    lon, lat = lax.axis_index("lon"), lax.axis_index("lat")
    count_lon, count_lat = lax.axis_size("lon"), lax.axis_size("lat")
    east, west = lax.rem(lon + 1, count_lon), lax.rem(lon + count_lon - 1, count_lon)
    south, north = lax.rem(lat + 1, count_lat), lax.rem(lat + count_lat - 1, count_lat)
    return {
        (row, column): {"lon": at_lon, "lat": at_lat}
        for row, at_lat in ((-1, north), (0, lat), (1, south))
        for column, at_lon in ((-1, west), (0, lon), (1, east))
        if (row, column) != (0, 0)
    }


class Halo:
    def __init__(self, own, west_in, east_in, west_out, east_out, send, recv, cuts):
        self.own, self.west_in, self.east_in = own, west_in, east_in
        self.west_out, self.east_out, self.send, self.recv = west_out, east_out, send, recv
        self.peers, self.rows, self.cuts, self.used = halo_peers(), own.shape[0] - 4, cuts, 0
        self.pairs, self.parts, self.top, self.bottom = self.rows // 2, [], [], []

    def copy(self, src, dst, peer):
        index = self.used
        self.used += 1
        copy = pltpu.make_async_remote_copy(
            src_ref=src, dst_ref=dst, send_sem=self.send.at[index], recv_sem=self.recv.at[index],
            device_id=self.peers[peer], device_id_type=MESH)
        copy.start()
        return copy

    def pack(self, first, values):
        pairs, channels = values.shape[0] // 2, values.shape[-1]
        split = values.reshape(pairs, 2, 16, channels)
        self.west_out[first : first + pairs] = split[:, :, :8].reshape(pairs, 16, channels).astype(jnp.bfloat16)
        self.east_out[first : first + pairs] = split[:, :, 8:].reshape(pairs, 16, channels).astype(jnp.bfloat16)

    def send_part(self, part):
        lo, hi = self.cuts[part], self.cuts[part + 1]
        self.parts.append([
            self.copy(self.east_out.at[lo:hi], self.west_in.at[lo + 1 : hi + 1], (0, 1)),
            self.copy(self.west_out.at[lo:hi], self.east_in.at[lo + 1 : hi + 1], (0, -1)),
        ])

    def send_north(self):
        rows, last = self.rows, self.pairs + 1
        self.bottom = [
            self.copy(self.own.at[2:4], self.own.at[rows + 2 : rows + 4], (-1, 0)),
            self.copy(self.east_out.at[0:1], self.west_in.at[last : last + 1], (-1, 1)),
            self.copy(self.west_out.at[0:1], self.east_in.at[last : last + 1], (-1, -1)),
        ]

    def send_south(self):
        rows, last = self.rows, self.pairs - 1
        self.top = [
            self.copy(self.own.at[rows : rows + 2], self.own.at[0:2], (1, 0)),
            self.copy(self.east_out.at[last : last + 1], self.west_in.at[0:1], (1, 1)),
            self.copy(self.west_out.at[last : last + 1], self.east_in.at[0:1], (1, -1)),
        ]

    def wait(self, copies):
        for copy in copies:
            copy.wait()

    def window(self, first):
        channels = self.own.shape[-1]
        pair = lax.div(first, 2)
        return jnp.concatenate([
            self.own[pl.ds(first, 8)].reshape(128, channels),
            self.west_in[pl.ds(pair, 4)].reshape(64, channels),
            self.east_in[pl.ds(pair, 4)].reshape(64, channels),
        ], axis=0)


def iota(shape, dim):
    return lax.broadcasted_iota(jnp.int32, shape, dim)


def lay_taps(filter_basis, half_widths, stage, taps):
    kernels, taps_lat, taps_lon, rows = filter_basis.shape
    allowed = jnp.abs(iota((taps_lon, rows), 0) - taps_lon // 2) <= half_widths[...]
    stage[...] = jnp.zeros_like(stage)
    taps[...] = jnp.zeros_like(taps)
    for b in range(kernels):
        for s in range(taps_lat):
            values = jnp.where(allowed, filter_basis[b, s].astype(jnp.float32), 0.0)
            stage[s * 32 : s * 32 + taps_lon, 0:rows] = values
        taps[b, 8 : 8 + stage.shape[1]] = stage[...].T


def base_rows(taps, b, first, rows, total_rows, backward):
    reach = 2
    near = taps[b, pl.ds(first, rows + 16)]
    lane = iota((rows, 256), 1)
    if not backward:
        source = iota((rows, 256), 0) + first + lax.div(lane, 32) - reach
        return jnp.where((source >= 0) & (source < total_rows), near[8 : 8 + rows], 0.0)
    chosen = jnp.zeros((rows, 256), jnp.float32)
    for s in range(5):
        start = 8 + reach - s
        chosen = jnp.where(lax.div(lane, 32) == s, near[start : start + rows], chosen)
    turned = (iota((256, 256), 0) + iota((256, 256), 1) == 144).astype(jnp.bfloat16)
    return jnp.dot(chosen.astype(jnp.bfloat16), turned, preferred_element_type=jnp.float32)


def lay_band(taps, base, moved, band, first, rows, total_rows, backward):
    kernels, blocks = taps.shape[0], rows // 4
    for b in range(kernels):
        base[b] = base_rows(taps, b, first, rows, total_rows, backward)

    def move(n, carry):
        for a in range(4):
            for b in range(kernels):
                row = jnp.broadcast_to(base[b, pl.ds(n * 4 + a, 1)], (16, 256))
                moved[a, n, b] = pltpu.roll(row, 0, 1, stride=1, stride_axis=0).astype(jnp.bfloat16)
        return carry

    lax.fori_loop(0, blocks, move, 0)
    place = iota((256, 256), 1)
    west, east = place - 128, place - 192
    own = lax.div(place, 16) * 32 + 8 + lax.rem(place, 16)
    side = jnp.where(place < 192, lax.div(west, 8) * 32 + lax.rem(west, 8), lax.div(east, 8) * 32 + 24 + lax.rem(east, 8))
    wanted = jnp.where(place < 128, own, side)
    for a in range(4):
        table = (iota((256, 256), 0) == wanted - 32 * a).astype(jnp.bfloat16)

        def place_rows(group, carry):
            at = pl.ds(group * 4, 4)
            rows_in = moved[a, at].reshape(4 * kernels * 16, 256)
            out = jnp.dot(rows_in, table, preferred_element_type=jnp.float32).astype(jnp.bfloat16)
            band[at, :, a] = out.reshape(4, kernels, 16, 256)
            return carry

        lax.fori_loop(0, blocks // 4, place_rows, 0)


def gelu_slope(values):
    cdf = 0.5 * (1.0 + lax.erf(values * math.sqrt(0.5)))
    return cdf + values * (jnp.exp(values * values * -0.5) * (1.0 / math.sqrt(2.0 * math.pi)))


def apply_blocks(band, halo, flat, part, channels, blocks):
    def block(step, carry):
        n = part * blocks + step
        out = jnp.dot(band[n].reshape(192, 256), halo.window(n * 4), preferred_element_type=jnp.float32).astype(jnp.bfloat16)
        at = pl.ds(pl.multiple_of(n * 64, 64), 64)
        for b in range(3):
            flat[at, b * channels : (b + 1) * channels] = out[b * 64 : (b + 1) * 64]
        return carry

    lax.fori_loop(0, blocks, block, 0)


def block_kernel(
    scale, features_hbm, filter_basis, half_widths, mixing_hbm, bias, cotangent_hbm, grad_hbm, mixing_out,
    own, west_in, east_in, west_out, east_out, send, recv,
    g_own, g_west_in, g_east_in, g_west_out, g_east_out, g_send, g_recv,
    mixing, cotangent, result, flat, local, stage, taps, base, moved, band, g_band, load_sem, store_sem, *sum_refs):
    rows, width, channels = cotangent.shape
    kernels = filter_basis.shape[0]
    total_rows = filter_basis.shape[3]
    parts, part_rows = 5, rows // 5
    blocks = part_rows // 4
    pairs = part_rows // 2
    loads = [
        pltpu.make_async_copy(features_hbm, own.at[2 : rows + 2], load_sem.at[0]),
        pltpu.make_async_copy(mixing_hbm, mixing, load_sem.at[1]),
        pltpu.make_async_copy(cotangent_hbm, cotangent, load_sem.at[2]),
    ]
    for load in loads:
        load.start()
    greet(list(halo_peers().values()) + sum_peers())
    cuts = [0] + [pairs * part + 1 for part in range(1, parts)] + [rows // 2]
    halo = Halo(own, west_in, east_in, west_out, east_out, send, recv, cuts)
    g_halo = Halo(g_own, g_west_in, g_east_in, g_west_out, g_east_out, g_send, g_recv, [pairs * part for part in range(parts + 1)])
    loads[0].wait()
    for part in range(parts):
        lo, hi = cuts[part], cuts[part + 1]
        halo.pack(lo, own[2 + 2 * lo : 2 + 2 * hi].astype(jnp.float32))
        halo.send_part(part)
        if part == 0:
            halo.send_north()
    halo.send_south()

    first = pl.multiple_of(lax.axis_index("lat") * rows, 8)
    lay_taps(filter_basis, half_widths, stage, taps)
    lay_band(taps, base, moved, band, first, rows, total_rows, False)
    lay_band(taps, base, moved, g_band, first, rows, total_rows, True)
    loads[1].wait()
    loads[2].wait()
    halo.wait(halo.top)
    cells = part_rows * width
    for part in range(parts):
        halo.wait(halo.parts[part])
        if part == parts - 1:
            halo.wait(halo.bottom)
        apply_blocks(band, halo, flat, part, channels, blocks)
        here = flat[part * cells : (part + 1) * cells]
        pre = jnp.dot(here, mixing[...], preferred_element_type=jnp.float32) + bias[...]
        at = part * part_rows
        cot = cotangent[at : at + part_rows].reshape(cells, channels).astype(jnp.float32)
        grad = cot * gelu_slope(pre)
        grad_rows = grad.reshape(part_rows, width, channels)
        grad = grad.astype(jnp.bfloat16)
        g_own[2 + at : 2 + at + part_rows] = grad.reshape(part_rows, width, channels)
        g_halo.pack(at // 2, grad_rows)
        g_halo.send_part(part)
        if part == 0:
            g_halo.send_north()
        if part == parts - 1:
            g_halo.send_south()
        outer = lax.dot_general(here, grad, (((0,), (0,)), ((), ())), preferred_element_type=jnp.float32)
        outer = outer.reshape(local.shape)
        if part == 0:
            local[...] = outer
        else:
            local[...] += outer

    work = SumOverAll(local, sum_refs, scale)
    steps = [work.start_core, work.finish_core_start_x, work.finish_x_start_z, work.finish_z_start_y, work.finish_y_start_gather]
    stores = []
    g_halo.wait(g_halo.top)
    g_halo.wait(g_halo.parts[0])
    for part in range(parts):
        steps[part]()
        if part < parts - 1:
            g_halo.wait(g_halo.parts[part + 1])
        else:
            g_halo.wait(g_halo.bottom)
        apply_blocks(g_band, g_halo, flat, part, channels, blocks)
        here = flat[part * cells : (part + 1) * cells]
        at = part * part_rows
        branch = cotangent[at : at + part_rows].reshape(cells, channels).astype(jnp.float32)
        for b in range(kernels):
            mix = mixing[b * channels : (b + 1) * channels]
            branch = branch + lax.dot_general(
                here[:, b * channels : (b + 1) * channels], mix, (((1,), (1,)), ((), ())), preferred_element_type=jnp.float32)
        result[at : at + part_rows] = branch.astype(jnp.bfloat16).reshape(part_rows, width, channels)
        stores.append(pltpu.make_async_copy(
            result.at[at : at + part_rows], grad_hbm.at[at : at + part_rows], store_sem.at[part]))
        stores[-1].start()
    work.finish_z_gather_x()
    work.finish_x_gather_core()
    work.finish(mixing_out)
    for store in stores:
        store.wait()


def halo_buffers(rows, channels, parts):
    side = pltpu.VMEM((rows // 2 + 2, 16, channels), jnp.bfloat16)
    out = pltpu.VMEM((rows // 2, 16, channels), jnp.bfloat16)
    copies = 2 * parts + 6
    return [
        pltpu.VMEM((rows + 4, 16, channels), jnp.bfloat16), side, side, out, out,
        pltpu.SemaphoreType.DMA((copies,)), pltpu.SemaphoreType.DMA((copies,)),
    ]


def per_device(features, filter_basis, half_widths, mixing, channel_bias, cotangent):
    rows, width, channels = features.shape
    kernels, taps_lat, taps_lon, total_rows = filter_basis.shape
    cells = rows * width
    cell_count = cells * lax.axis_size("lat") * lax.axis_size("lon")
    sum_rows = kernels * channels // (2 * SIZE_X)
    blocks = rows // 4
    lanes = -(-total_rows // 128) * 128
    anywhere, vmem = pl.BlockSpec(memory_space=pl.ANY), pl.BlockSpec(memory_space=pltpu.VMEM)
    band = pltpu.VMEM((blocks, kernels, 4, 16, 256), jnp.bfloat16)
    return pl.pallas_call(
        lambda *refs: block_kernel(math.sqrt(cell_count), *refs),
        out_shape=(
            jax.ShapeDtypeStruct((rows, width, channels), jnp.bfloat16),
            jax.ShapeDtypeStruct((kernels * channels, channels), jnp.bfloat16),
        ),
        in_specs=[anywhere, vmem, vmem, anywhere, vmem, anywhere],
        out_specs=(anywhere, vmem),
        scratch_shapes=[
            *halo_buffers(rows, channels, 5),
            *halo_buffers(rows, channels, 5),
            pltpu.VMEM((kernels * channels, channels), jnp.bfloat16),
            pltpu.VMEM((rows, width, channels), jnp.bfloat16),
            pltpu.VMEM((rows, width, channels), jnp.bfloat16),
            pltpu.VMEM((cells, kernels * channels), jnp.bfloat16),
            pltpu.VMEM((2, SIZE_X, sum_rows, channels), jnp.float32),
            pltpu.VMEM((256, lanes), jnp.float32),
            pltpu.VMEM((kernels, lanes + 16, 256), jnp.float32),
            pltpu.VMEM((kernels, rows, 256), jnp.float32),
            pltpu.VMEM((4, blocks, kernels, 16, 256), jnp.bfloat16),
            band,
            band,
            pltpu.SemaphoreType.DMA((3,)),
            pltpu.SemaphoreType.DMA((5,)),
            *sum_buffers(sum_rows, channels),
        ],
        compiler_params=pltpu.CompilerParams(
            collective_id=0, has_side_effects=True, vmem_limit_bytes=48 * 1024 * 1024),
    )(features, filter_basis, half_widths.reshape(1, total_rows), mixing, channel_bias.reshape(1, channels), cotangent)


def solution(mesh):
    return jax.shard_map(
        per_device,
        mesh=mesh,
        in_specs=(P("lat", "lon", None), P(), P(), P(), P(), P("lat", "lon", None)),
        out_specs=(P("lat", "lon", None), P()),
        check_vma=False,
    )
```

```python
import math

import jax
import jax.numpy as jnp
from jax import lax
from jax.experimental import pallas as pl
from jax.experimental.pallas import tpu as pltpu
from jax.sharding import PartitionSpec as P

MESH = pl.DeviceIdType.MESH
SIZE_X_LO, SIZE_Z, SIZE_Y = 2, 8, 8
SIZE_X = 4


def position():
    lon, lat = lax.axis_index("lon"), lax.axis_index("lat")
    x = lax.div(lat, 2) * SIZE_X_LO + lax.div(lon, SIZE_Z * SIZE_Y)
    z = lax.rem(lax.div(lon, SIZE_Y), SIZE_Z)
    return x, z, lax.rem(lon, SIZE_Y), lax.rem(lat, 2)


def device(x, z, y, core):
    lon = (lax.rem(x, SIZE_X_LO) * SIZE_Z + z) * SIZE_Y + y
    return {"lon": lon, "lat": lax.div(x, SIZE_X_LO) * 2 + core}


def sum_peers():
    x, z, y, core = position()
    peers = [device(x, z, y, 1 - core)]
    peers += [device(lax.rem(x + d, SIZE_X), z, y, core) for d in range(1, SIZE_X)]
    peers += [device(x, lax.rem(z + d, SIZE_Z), y, core) for d in range(1, SIZE_Z)]
    peers += [device(x, z, lax.rem(y + d, SIZE_Y), core) for d in range(1, SIZE_Y)]
    return peers


def greet(peers):
    barrier = pltpu.get_barrier_semaphore()
    for peer in peers:
        pl.semaphore_signal(barrier, inc=1, device_id=peer, device_id_type=MESH)


def await_greetings(count):
    pl.semaphore_wait(pltpu.get_barrier_semaphore(), count)


SHARE = 4
Y_ORDER = (4, 3, 5, 2, 6, 1, 7, 0)
GATHER_ORDER = (0, 1, 7, 2, 6, 3, 5, 4)


def tile_count(part_rows, channels):
    tiles = (part_rows // 16) * (channels // 128)
    assert (SIZE_Y - 1) * SHARE <= tiles + 1 <= SIZE_Y * SHARE
    return tiles


def sum_buffers():
    pieces = (SIZE_Y, SIZE_X, SHARE, 16, 128)
    copies = SIZE_Y + 2 * SIZE_Y * (SIZE_X - 1) + 2 * (SIZE_Y - 1) + SIZE_Z - 1 + SIZE_X
    return [
        pltpu.VMEM((2, *pieces), jnp.float32),
        pltpu.VMEM(pieces, jnp.float32),
        pltpu.VMEM(pieces, jnp.bfloat16),
        pltpu.VMEM((SIZE_X - 1, SIZE_Y, SHARE, 16, 128), jnp.bfloat16),
        pltpu.VMEM((SIZE_Y - 1, SHARE, 16, 128), jnp.bfloat16),
        pltpu.VMEM((SIZE_Y - 1, SHARE, 16, 128), jnp.bfloat16),
        pltpu.VMEM((SIZE_Z, SHARE, 16, 128), jnp.bfloat16),
        pltpu.VMEM((2, SIZE_X, SIZE_Y, SHARE, 16, 128), jnp.bfloat16),
        pltpu.SemaphoreType.DMA((copies,)),
        pltpu.SemaphoreType.DMA((copies,)),
    ]


class SumOverAll:
    def __init__(self, rows, channels, buffers, scale):
        (self.local, self.half, self.x_out, self.x_in, self.y_out, self.y_in, self.z_all, self.done, self.send, self.recv) = buffers
        self.rows, self.lanes, self.tiles, self.scale = rows, channels // 128, tile_count(rows, channels), scale
        self.x, self.z, self.y, self.core = position()
        self.used, self.sent = 0, []

    def copy(self, src, dst, peer):
        index = self.used
        self.used += 1
        copy = pltpu.make_async_remote_copy(
            src_ref=src, dst_ref=dst, send_sem=self.send.at[index], recv_sem=self.recv.at[index],
            device_id=peer, device_id_type=MESH)
        copy.start()
        self.sent.append(copy)
        return copy

    def other_core(self):
        return device(self.x, self.z, self.y, 1 - self.core)

    def other_x(self, d):
        return device(lax.rem(self.x + d, SIZE_X), self.z, self.y, self.core)

    def other_y(self, d):
        return device(self.x, self.z, lax.rem(self.y + d, SIZE_Y), self.core)

    def other_z(self, d):
        return device(self.x, lax.rem(self.z + d, SIZE_Z), self.y, self.core)

    def places(self, core, part):
        for t in range(self.tiles):
            row = (core * SIZE_X + part) * self.rows + t // self.lanes * 16
            lane = t % self.lanes * 128
            yield t // SHARE, t % SHARE, slice(row, row + 16), slice(lane, lane + 128)

    def clear(self):
        self.local[:, SIZE_Y - 2 :] = jnp.zeros_like(self.local[:, SIZE_Y - 2 :])

    def lay(self, values, more):
        for core in range(2):
            for part in range(SIZE_X):
                for y, slot, rows, lanes in self.places(core, part):
                    self.local[core, y, part, slot] = values[rows, lanes] + more[rows, lanes]

    def start_core(self):
        self.from_core = {}
        for d in Y_ORDER:
            y = lax.rem(self.y + d, SIZE_Y)
            self.from_core[d] = self.copy(self.local.at[1 - self.core, y], self.half.at[y], self.other_core())

    def core_to_x(self):
        self.from_x = {}
        for d in Y_ORDER:
            y = lax.rem(self.y + d, SIZE_Y)
            self.from_core[d].wait_recv()
            total = self.half[y] + self.local[self.core, y]
            self.half[y] = total
            self.x_out[y] = total.astype(jnp.bfloat16)
            self.from_x[d] = [
                self.copy(self.x_out.at[y, lax.rem(self.x + e, SIZE_X)], self.x_in.at[e - 1, y], self.other_x(e))
                for e in (2, 1, 3)
            ]

    def x_to_y(self):
        self.from_y = []
        for d in Y_ORDER:
            y = lax.rem(self.y + d, SIZE_Y)
            total = self.half[y, self.x]
            for copy in self.from_x[d]:
                copy.wait_recv()
            for e in range(SIZE_X - 1):
                total = total + self.x_in[e, y].astype(jnp.float32)
            if d:
                self.y_out[d - 1] = total.astype(jnp.bfloat16)
                self.from_y.append(self.copy(self.y_out.at[d - 1], self.y_in.at[d - 1], self.other_y(d)))
            else:
                self.half[y, self.x] = total

    def y_to_z(self):
        total = self.half[self.y, self.x]
        for copy in self.from_y:
            copy.wait_recv()
        for d in range(SIZE_Y - 1):
            total = total + self.y_in[d].astype(jnp.float32)
        self.z_all[self.z] = total.astype(jnp.bfloat16)
        piece = self.z_all.at[self.z]
        self.from_z = [self.copy(piece, piece, self.other_z(d)) for d in (4, 3, 5, 2, 6, 1, 7)]

    def spread_x(self, d):
        y = lax.rem(self.y + SIZE_Y - d, SIZE_Y)
        piece = self.done.at[self.core, self.x, y]
        for e in (2, 1, 3):
            self.gathered[e].append(self.copy(piece, piece, self.other_x(e)))

    def z_to_gather(self):
        for copy in self.from_z:
            copy.wait_recv()
        total = self.z_all[0].astype(jnp.float32)
        for other in range(1, SIZE_Z):
            total = total + self.z_all[other].astype(jnp.float32)
        self.done[self.core, self.x, self.y] = (total / self.scale).astype(jnp.bfloat16)
        piece = self.done.at[self.core, self.x, self.y]
        self.y_gathered = {d: self.copy(piece, piece, self.other_y(d)) for d in (4, 3, 5, 2, 6, 1, 7)}
        self.gathered = {e: [] for e in range(1, SIZE_X)}
        self.spread_x(0)

    def gather_y(self):
        for d in GATHER_ORDER[1:]:
            self.y_gathered[d].wait_recv()
            self.spread_x(d)
        self.spread_core(0)

    def spread_core(self, e):
        part = self.done.at[self.core, lax.rem(self.x + SIZE_X - e, SIZE_X)]
        self.copy(part, part, self.other_core())

    def gather_x(self):
        for e in (1, 3, 2):
            for copy in self.gathered[e]:
                copy.wait_recv()
            self.spread_core(e)

    def finish(self, out):
        for copy in self.sent[-SIZE_X:]:
            copy.wait_recv()
        for core in range(2):
            for part in range(SIZE_X):
                for y, slot, rows, lanes in self.places(core, part):
                    out[rows, lanes] = self.done[core, part, y, slot]
        for copy in self.sent:
            copy.wait_send()


def halo_peers():
    lon, lat = lax.axis_index("lon"), lax.axis_index("lat")
    count_lon, count_lat = lax.axis_size("lon"), lax.axis_size("lat")
    east, west = lax.rem(lon + 1, count_lon), lax.rem(lon + count_lon - 1, count_lon)
    south, north = lax.rem(lat + 1, count_lat), lax.rem(lat + count_lat - 1, count_lat)
    return {
        (row, column): {"lon": at_lon, "lat": at_lat}
        for row, at_lat in ((-1, north), (0, lat), (1, south))
        for column, at_lon in ((-1, west), (0, lon), (1, east))
        if (row, column) != (0, 0)
    }


class Halo:
    def __init__(self, own, west_in, east_in, west_out, east_out, send, recv, cuts):
        self.own, self.west_in, self.east_in = own, west_in, east_in
        self.west_out, self.east_out, self.send, self.recv = west_out, east_out, send, recv
        self.peers, self.rows, self.cuts, self.used = halo_peers(), own.shape[0] - 4, cuts, 0
        self.pairs, self.parts, self.top, self.bottom = self.rows // 2, [], [], []

    def copy(self, src, dst, peer):
        index = self.used
        self.used += 1
        copy = pltpu.make_async_remote_copy(
            src_ref=src, dst_ref=dst, send_sem=self.send.at[index], recv_sem=self.recv.at[index],
            device_id=self.peers[peer], device_id_type=MESH)
        copy.start()
        return copy

    def pack(self, first, values):
        pairs, channels = values.shape[0] // 2, values.shape[-1]
        split = values.reshape(pairs, 2, 16, channels)
        self.west_out[first : first + pairs] = split[:, :, :8].reshape(pairs, 16, channels).astype(jnp.bfloat16)
        self.east_out[first : first + pairs] = split[:, :, 8:].reshape(pairs, 16, channels).astype(jnp.bfloat16)

    def send_part(self, part):
        lo, hi = self.cuts[part], self.cuts[part + 1]
        self.parts.append([
            self.copy(self.east_out.at[lo:hi], self.west_in.at[lo + 1 : hi + 1], (0, 1)),
            self.copy(self.west_out.at[lo:hi], self.east_in.at[lo + 1 : hi + 1], (0, -1)),
        ])

    def send_north(self):
        rows, last = self.rows, self.pairs + 1
        self.bottom = [
            self.copy(self.own.at[2:4], self.own.at[rows + 2 : rows + 4], (-1, 0)),
            self.copy(self.east_out.at[0:1], self.west_in.at[last : last + 1], (-1, 1)),
            self.copy(self.west_out.at[0:1], self.east_in.at[last : last + 1], (-1, -1)),
        ]

    def send_south(self):
        rows, last = self.rows, self.pairs - 1
        self.top = [
            self.copy(self.own.at[rows : rows + 2], self.own.at[0:2], (1, 0)),
            self.copy(self.east_out.at[last : last + 1], self.west_in.at[0:1], (1, 1)),
            self.copy(self.west_out.at[last : last + 1], self.east_in.at[0:1], (1, -1)),
        ]

    def wait(self, copies):
        for copy in copies:
            copy.wait()

    def window(self, first):
        channels = self.own.shape[-1]
        pair = first // 2
        return jnp.concatenate([
            self.own[first : first + 8].reshape(128, channels),
            self.west_in[pair : pair + 4].reshape(64, channels),
            self.east_in[pair : pair + 4].reshape(64, channels),
        ], axis=0)


def iota(shape, dim):
    return lax.broadcasted_iota(jnp.int32, shape, dim)


def lay_taps(filter_basis, half_widths, stage, taps):
    taps_lat, taps_lon, kernels, rows = filter_basis.shape
    allowed = jnp.abs(iota((taps_lon, rows), 0) - taps_lon // 2) <= half_widths[...].reshape(1, rows)
    stage[...] = jnp.zeros_like(stage)
    taps[...] = jnp.zeros_like(taps)
    for b in range(kernels):
        for s in range(taps_lat):
            values = jnp.where(allowed, filter_basis[s].astype(jnp.float32)[:, b], 0.0)
            stage[s * 32 : s * 32 + taps_lon, 0:rows] = values
        taps[b, 8 : 8 + stage.shape[1]] = stage[...].T


def base_rows(taps, b, first, rows, total_rows, backward):
    reach = 2
    near = taps[b, pl.ds(first, rows + 16)]
    lane = iota((rows, 256), 1)
    if not backward:
        source = iota((rows, 256), 0) + first + lax.div(lane, 32) - reach
        return jnp.where((source >= 0) & (source < total_rows), near[8 : 8 + rows], 0.0)
    chosen = jnp.zeros((rows, 256), jnp.float32)
    for s in range(5):
        start = 8 + reach - s
        chosen = jnp.where(lax.div(lane, 32) == s, near[start : start + rows], chosen)
    turned = (iota((256, 256), 0) + iota((256, 256), 1) == 144).astype(jnp.bfloat16)
    return jnp.dot(chosen.astype(jnp.bfloat16), turned, preferred_element_type=jnp.float32)


def lay_band(taps, base, moved, band, first, rows, total_rows, backward):
    kernels, blocks = taps.shape[0], rows // 4
    for b in range(kernels):
        base[b] = base_rows(taps, b, first, rows, total_rows, backward)

    def move(n, carry):
        for a in range(4):
            for b in range(kernels):
                row = jnp.broadcast_to(base[b, pl.ds(n * 4 + a, 1)], (16, 256))
                moved[a, n, b] = pltpu.roll(row, 0, 1, stride=1, stride_axis=0).astype(jnp.bfloat16)
        return carry

    lax.fori_loop(0, blocks, move, 0)
    place = iota((256, 256), 1)
    west, east = place - 128, place - 192
    own = lax.div(place, 16) * 32 + 8 + lax.rem(place, 16)
    side = jnp.where(place < 192, lax.div(west, 8) * 32 + lax.rem(west, 8), lax.div(east, 8) * 32 + 24 + lax.rem(east, 8))
    wanted = jnp.where(place < 128, own, side)
    for a in range(4):
        table = (iota((256, 256), 0) == wanted - 32 * a).astype(jnp.bfloat16)

        rows_in = moved[a].reshape(blocks * kernels * 16, 256)
        out = jnp.dot(rows_in, table, preferred_element_type=jnp.float32).astype(jnp.bfloat16)
        band[:, :, a] = out.reshape(blocks, kernels, 16, 256)


def gelu_slope(values):
    cdf = 0.5 * (1.0 + lax.erf(values * math.sqrt(0.5)))
    return cdf + values * (jnp.exp(values * values * -0.5) * (1.0 / math.sqrt(2.0 * math.pi)))


def apply_blocks(band, halo, flat, part, channels, blocks):
    for n in range(part * blocks, (part + 1) * blocks):
        out = jnp.dot(band[n].reshape(192, 256), halo.window(n * 4), preferred_element_type=jnp.float32).astype(jnp.bfloat16)
        for b in range(3):
            flat[n * 64 : (n + 1) * 64, b * channels : (b + 1) * channels] = out[b * 64 : (b + 1) * 64]


def block_kernel(
    scale, features_hbm, filter_hbm, half_widths, mixing_hbm, bias, cotangent_hbm, grad_hbm, mixing_out,
    own, west_in, east_in, west_out, east_out, send, recv,
    g_own, g_west_in, g_east_in, g_west_out, g_east_out, g_send, g_recv,
    mixing, cotangent, result, flat, local, stage, taps, base, moved, band, g_band, filter_basis, load_sem, store_sem, *sum_refs):
    rows, width, channels = cotangent.shape
    kernels, total_rows = filter_basis.shape[2:]
    parts, part_rows = 5, rows // 5
    blocks = part_rows // 4
    pairs = part_rows // 2
    loads = [
        pltpu.make_async_copy(features_hbm, own.at[2 : rows + 2], load_sem.at[0]),
        pltpu.make_async_copy(filter_hbm, filter_basis, load_sem.at[3]),
        pltpu.make_async_copy(mixing_hbm, mixing, load_sem.at[1]),
        pltpu.make_async_copy(cotangent_hbm, cotangent, load_sem.at[2]),
    ]
    for load in loads:
        load.start()
    peers = list(halo_peers().values()) + sum_peers()
    greet(peers)
    work = SumOverAll(mixing.shape[0] // (2 * SIZE_X), channels, sum_refs, scale)
    cuts = [0] + [pairs * part + 1 for part in range(1, parts)] + [rows // 2]
    halo = Halo(own, west_in, east_in, west_out, east_out, send, recv, cuts)
    g_halo = Halo(g_own, g_west_in, g_east_in, g_west_out, g_east_out, g_send, g_recv, [pairs * part for part in range(parts + 1)])
    loads[0].wait()
    for part in range(parts):
        lo, hi = cuts[part], cuts[part + 1]
        halo.pack(lo, own[2 + 2 * lo : 2 + 2 * hi].astype(jnp.float32))
    work.clear()
    await_greetings(len(peers))
    halo.send_north()
    for part in range(parts):
        halo.send_part(part)
    halo.send_south()

    first = pl.multiple_of(lax.axis_index("lat") * rows, 8)
    loads[1].wait()
    lay_taps(filter_basis, half_widths, stage, taps)
    lay_band(taps, base, moved, band, first, rows, total_rows, False)
    loads[2].wait()
    loads[3].wait()
    halo.wait(halo.top)
    cells = part_rows * width
    for part in range(parts):
        halo.wait(halo.parts[part])
        if part == parts - 1:
            halo.wait(halo.bottom)
        apply_blocks(band, halo, flat, part, channels, blocks)
        here = flat[part * cells : (part + 1) * cells]
        pre = jnp.dot(here, mixing[...], preferred_element_type=jnp.float32) + bias[...].reshape(1, channels)
        at = part * part_rows
        cot = cotangent[at : at + part_rows].reshape(cells, channels).astype(jnp.float32)
        grad = cot * gelu_slope(pre)
        grad_rows = grad.reshape(part_rows, width, channels)
        grad = grad.astype(jnp.bfloat16)
        g_own[2 + at : 2 + at + part_rows] = grad.reshape(part_rows, width, channels)
        g_halo.pack(at // 2, grad_rows)
        g_halo.send_part(part)
        if part == 0:
            g_halo.send_north()
        if part == parts - 1:
            g_halo.send_south()
        outer = lax.dot_general(here, grad, (((0,), (0,)), ((), ())), preferred_element_type=jnp.float32)
        if part == 0:
            local[...] = outer
        elif part < parts - 1:
            local[...] += outer
        else:
            work.lay(outer, local)

    work.start_core()
    work.core_to_x()
    lay_band(taps, base, moved, g_band, first, rows, total_rows, True)
    work.x_to_y()
    steps = {1: work.y_to_z, 3: work.z_to_gather, 4: work.gather_y}
    stores = []
    g_halo.wait(g_halo.top)
    g_halo.wait(g_halo.parts[0])
    for part in range(parts):
        if part in steps:
            steps[part]()
        if part < parts - 1:
            g_halo.wait(g_halo.parts[part + 1])
        else:
            g_halo.wait(g_halo.bottom)
        apply_blocks(g_band, g_halo, flat, part, channels, blocks)
        here = flat[part * cells : (part + 1) * cells]
        at = part * part_rows
        branch = cotangent[at : at + part_rows].reshape(cells, channels).astype(jnp.float32)
        for b in range(kernels):
            mix = mixing[b * channels : (b + 1) * channels]
            branch = branch + lax.dot_general(
                here[:, b * channels : (b + 1) * channels], mix, (((1,), (1,)), ((), ())), preferred_element_type=jnp.float32)
        result[at : at + part_rows] = branch.astype(jnp.bfloat16).reshape(part_rows, width, channels)
        stores.append(pltpu.make_async_copy(
            result.at[at : at + part_rows], grad_hbm.at[at : at + part_rows], store_sem.at[part]))
        stores[-1].start()
    work.gather_x()
    work.finish(mixing_out)
    for store in stores:
        store.wait()


def halo_buffers(rows, channels, parts):
    side = pltpu.VMEM((rows // 2 + 2, 16, channels), jnp.bfloat16)
    out = pltpu.VMEM((rows // 2, 16, channels), jnp.bfloat16)
    copies = 2 * parts + 6
    return [
        pltpu.VMEM((rows + 4, 16, channels), jnp.bfloat16), side, side, out, out,
        pltpu.SemaphoreType.DMA((copies,)), pltpu.SemaphoreType.DMA((copies,)),
    ]


def per_device(features, filter_basis, half_widths, mixing, channel_bias, cotangent):
    rows, width, channels = features.shape
    kernels, taps_lat, taps_lon, total_rows = filter_basis.shape
    cells = rows * width
    cell_count = cells * lax.axis_size("lat") * lax.axis_size("lon")
    blocks = rows // 4
    lanes = -(-total_rows // 128) * 128
    anywhere, vmem = pl.BlockSpec(memory_space=pltpu.HBM), pl.BlockSpec(memory_space=pltpu.VMEM)
    band = pltpu.VMEM((blocks, kernels, 4, 16, 256), jnp.bfloat16)
    return pl.pallas_call(
        lambda *refs: block_kernel(math.sqrt(cell_count), *refs),
        out_shape=(
            jax.ShapeDtypeStruct((rows, width, channels), jnp.bfloat16),
            jax.ShapeDtypeStruct((kernels * channels, channels), jnp.bfloat16),
        ),
        in_specs=[anywhere, anywhere, vmem, anywhere, vmem, anywhere],
        out_specs=(anywhere, vmem),
        scratch_shapes=[
            *halo_buffers(rows, channels, 5),
            *halo_buffers(rows, channels, 5),
            pltpu.VMEM((kernels * channels, channels), jnp.bfloat16),
            pltpu.VMEM((rows, width, channels), jnp.bfloat16),
            pltpu.VMEM((rows, width, channels), jnp.bfloat16),
            pltpu.VMEM((cells, kernels * channels), jnp.bfloat16),
            pltpu.VMEM((kernels * channels, channels), jnp.float32),
            pltpu.VMEM((256, lanes), jnp.float32),
            pltpu.VMEM((kernels, lanes + 16, 256), jnp.float32),
            pltpu.VMEM((kernels, rows, 256), jnp.float32),
            pltpu.VMEM((4, blocks, kernels, 16, 256), jnp.bfloat16),
            band,
            band,
            pltpu.VMEM((taps_lat, taps_lon, kernels, total_rows), jnp.bfloat16),
            pltpu.SemaphoreType.DMA((4,)),
            pltpu.SemaphoreType.DMA((5,)),
            *sum_buffers(),
        ],
        compiler_params=pltpu.CompilerParams(
            collective_id=0, has_side_effects=True, vmem_limit_bytes=56 * 1024 * 1024),
    )(features, filter_basis.transpose(1, 2, 0, 3), half_widths, mixing, channel_bias, cotangent)


def solution(mesh):
    return jax.shard_map(
        per_device,
        mesh=mesh,
        in_specs=(P("lat", "lon", None), P(), P(), P(), P(), P("lat", "lon", None)),
        out_specs=(P("lat", "lon", None), P()),
        check_vma=False,
    )
```

```python
import math

import jax
import jax.numpy as jnp
from jax import lax
from jax.experimental import pallas as pl
from jax.experimental.pallas import tpu as pltpu
from jax.sharding import PartitionSpec as P

MESH = pl.DeviceIdType.MESH
SIZE_X_LO, SIZE_Z, SIZE_Y = 2, 8, 8
SIZE_X = 4


def position():
    lon, lat = lax.axis_index("lon"), lax.axis_index("lat")
    x = lax.div(lat, 2) * SIZE_X_LO + lax.div(lon, SIZE_Z * SIZE_Y)
    z = lax.rem(lax.div(lon, SIZE_Y), SIZE_Z)
    return x, z, lax.rem(lon, SIZE_Y), lax.rem(lat, 2)


def device(x, z, y, core):
    lon = (lax.rem(x, SIZE_X_LO) * SIZE_Z + z) * SIZE_Y + y
    return {"lon": lon, "lat": lax.div(x, SIZE_X_LO) * 2 + core}


def sum_peers():
    x, z, y, core = position()
    peers = [device(x, z, y, 1 - core)]
    peers += [device(lax.rem(x + d, SIZE_X), z, y, core) for d in range(1, SIZE_X)]
    peers += [device(x, lax.rem(z + d, SIZE_Z), y, core) for d in range(1, SIZE_Z)]
    peers += [device(x, z, lax.rem(y + d, SIZE_Y), core) for d in range(1, SIZE_Y)]
    return peers


def greet(peers):
    barrier = pltpu.get_barrier_semaphore()
    for peer in peers:
        pl.semaphore_signal(barrier, inc=1, device_id=peer, device_id_type=MESH)


def await_greetings(count):
    pl.semaphore_wait(pltpu.get_barrier_semaphore(), count)


SHARE = 4
Y_ORDER = (4, 3, 5, 2, 6, 1, 7, 0)
GATHER_ORDER = (0, 1, 7, 2, 6, 3, 5, 4)


def tile_count(part_rows, channels):
    tiles = (part_rows // 16) * (channels // 128)
    assert (SIZE_Y - 1) * SHARE <= tiles + 1 <= SIZE_Y * SHARE
    return tiles


def sum_buffers():
    pieces = (SIZE_Y, SIZE_X, SHARE, 16, 128)
    copies = SIZE_Y + 2 * SIZE_Y * (SIZE_X - 1) + 2 * (SIZE_Y - 1) + SIZE_Z - 1 + SIZE_X
    return [
        pltpu.VMEM((2, *pieces), jnp.float32),
        pltpu.VMEM(pieces, jnp.float32),
        pltpu.VMEM(pieces, jnp.bfloat16),
        pltpu.VMEM((SIZE_X - 1, SIZE_Y, SHARE, 16, 128), jnp.bfloat16),
        pltpu.VMEM((SIZE_Y - 1, SHARE, 16, 128), jnp.bfloat16),
        pltpu.VMEM((SIZE_Y - 1, SHARE, 16, 128), jnp.bfloat16),
        pltpu.VMEM((SIZE_Z, SHARE, 16, 128), jnp.bfloat16),
        pltpu.VMEM((2, SIZE_X, SIZE_Y, SHARE, 16, 128), jnp.bfloat16),
        pltpu.SemaphoreType.DMA((copies,)),
        pltpu.SemaphoreType.DMA((copies,)),
    ]


class SumOverAll:
    def __init__(self, rows, channels, buffers, scale):
        (self.local, self.half, self.x_out, self.x_in, self.y_out, self.y_in, self.z_all, self.done, self.send, self.recv) = buffers
        self.rows, self.lanes, self.tiles, self.scale = rows, channels // 128, tile_count(rows, channels), scale
        self.x, self.z, self.y, self.core = position()
        self.used, self.sent = 0, []

    def copy(self, src, dst, peer):
        index = self.used
        self.used += 1
        copy = pltpu.make_async_remote_copy(
            src_ref=src, dst_ref=dst, send_sem=self.send.at[index], recv_sem=self.recv.at[index],
            device_id=peer, device_id_type=MESH)
        copy.start()
        self.sent.append(copy)
        return copy

    def other_core(self):
        return device(self.x, self.z, self.y, 1 - self.core)

    def other_x(self, d):
        return device(lax.rem(self.x + d, SIZE_X), self.z, self.y, self.core)

    def other_y(self, d):
        return device(self.x, self.z, lax.rem(self.y + d, SIZE_Y), self.core)

    def other_z(self, d):
        return device(self.x, lax.rem(self.z + d, SIZE_Z), self.y, self.core)

    def places(self, core, part):
        for t in range(self.tiles):
            row = (core * SIZE_X + part) * self.rows + t // self.lanes * 16
            lane = t % self.lanes * 128
            yield t // SHARE, t % SHARE, slice(row, row + 16), slice(lane, lane + 128)

    def clear(self):
        self.local[:, SIZE_Y - 2 :] = jnp.zeros_like(self.local[:, SIZE_Y - 2 :])

    def lay(self, values, more):
        for core in range(2):
            for part in range(SIZE_X):
                for y, slot, rows, lanes in self.places(core, part):
                    self.local[core, y, part, slot] = values[rows, lanes] + more[rows, lanes]

    def start_core(self):
        self.from_core = {}
        for d in Y_ORDER:
            y = lax.rem(self.y + d, SIZE_Y)
            self.from_core[d] = self.copy(self.local.at[1 - self.core, y], self.half.at[y], self.other_core())

    def core_to_x(self):
        self.from_x = {}
        for d in Y_ORDER:
            y = lax.rem(self.y + d, SIZE_Y)
            self.from_core[d].wait_recv()
            total = self.half[y] + self.local[self.core, y]
            self.half[y] = total
            self.x_out[y] = total.astype(jnp.bfloat16)
            self.from_x[d] = [
                self.copy(self.x_out.at[y, lax.rem(self.x + e, SIZE_X)], self.x_in.at[e - 1, y], self.other_x(e))
                for e in (2, 1, 3)
            ]

    def x_to_y(self):
        self.from_y = []
        for d in Y_ORDER:
            y = lax.rem(self.y + d, SIZE_Y)
            total = self.half[y, self.x]
            for copy in self.from_x[d]:
                copy.wait_recv()
            for e in range(SIZE_X - 1):
                total = total + self.x_in[e, y].astype(jnp.float32)
            if d:
                self.y_out[d - 1] = total.astype(jnp.bfloat16)
                self.from_y.append(self.copy(self.y_out.at[d - 1], self.y_in.at[d - 1], self.other_y(d)))
            else:
                self.half[y, self.x] = total

    def y_to_z(self):
        total = self.half[self.y, self.x]
        for copy in self.from_y:
            copy.wait_recv()
        for d in range(SIZE_Y - 1):
            total = total + self.y_in[d].astype(jnp.float32)
        self.z_all[self.z] = total.astype(jnp.bfloat16)
        piece = self.z_all.at[self.z]
        self.from_z = [self.copy(piece, piece, self.other_z(d)) for d in (4, 3, 5, 2, 6, 1, 7)]

    def spread_x(self, d):
        y = lax.rem(self.y + SIZE_Y - d, SIZE_Y)
        piece = self.done.at[self.core, self.x, y]
        for e in (2, 1, 3):
            self.gathered[e].append(self.copy(piece, piece, self.other_x(e)))

    def z_to_gather(self):
        for copy in self.from_z:
            copy.wait_recv()
        total = self.z_all[0].astype(jnp.float32)
        for other in range(1, SIZE_Z):
            total = total + self.z_all[other].astype(jnp.float32)
        self.done[self.core, self.x, self.y] = (total / self.scale).astype(jnp.bfloat16)
        piece = self.done.at[self.core, self.x, self.y]
        self.y_gathered = {d: self.copy(piece, piece, self.other_y(d)) for d in (4, 3, 5, 2, 6, 1, 7)}
        self.gathered = {e: [] for e in range(1, SIZE_X)}
        self.spread_x(0)

    def gather_y(self):
        for d in GATHER_ORDER[1:]:
            self.y_gathered[d].wait_recv()
            self.spread_x(d)
        self.spread_core(0)

    def spread_core(self, e):
        part = self.done.at[self.core, lax.rem(self.x + SIZE_X - e, SIZE_X)]
        self.copy(part, part, self.other_core())

    def gather_x(self):
        for e in (1, 3, 2):
            for copy in self.gathered[e]:
                copy.wait_recv()
            self.spread_core(e)

    def finish(self, out):
        for copy in self.sent[-SIZE_X:]:
            copy.wait_recv()
        for core in range(2):
            for part in range(SIZE_X):
                for y, slot, rows, lanes in self.places(core, part):
                    out[rows, lanes] = self.done[core, part, y, slot]
        for copy in self.sent:
            copy.wait_send()


def halo_peers():
    lon, lat = lax.axis_index("lon"), lax.axis_index("lat")
    count_lon, count_lat = lax.axis_size("lon"), lax.axis_size("lat")
    east, west = lax.rem(lon + 1, count_lon), lax.rem(lon + count_lon - 1, count_lon)
    south, north = lax.rem(lat + 1, count_lat), lax.rem(lat + count_lat - 1, count_lat)
    return {
        (row, column): {"lon": at_lon, "lat": at_lat}
        for row, at_lat in ((-1, north), (0, lat), (1, south))
        for column, at_lon in ((-1, west), (0, lon), (1, east))
        if (row, column) != (0, 0)
    }


class Halo:
    def __init__(self, own, west_in, east_in, west_out, east_out, send, recv, cuts):
        self.own, self.west_in, self.east_in = own, west_in, east_in
        self.west_out, self.east_out, self.send, self.recv = west_out, east_out, send, recv
        self.peers, self.rows, self.cuts, self.used = halo_peers(), own.shape[0] - 4, cuts, 0
        self.pairs, self.parts, self.top, self.bottom, self.sent = self.rows // 2, [], [], [], []

    def copy(self, src, dst, peer):
        index = self.used
        self.used += 1
        copy = pltpu.make_async_remote_copy(
            src_ref=src, dst_ref=dst, send_sem=self.send.at[index], recv_sem=self.recv.at[index],
            device_id=self.peers[peer], device_id_type=MESH)
        copy.start()
        self.sent.append(copy)
        return copy

    def left(self, part):
        for copy in self.parts[part]:
            copy.wait_send()
            self.sent = [other for other in self.sent if other is not copy]

    def drain(self):
        for copy in self.sent:
            copy.wait_send()

    def pack(self, first, values):
        pairs, channels = values.shape[0] // 2, values.shape[-1]
        split = values.reshape(pairs, 2, 16, channels)
        self.west_out[first : first + pairs] = split[:, :, :8].reshape(pairs, 16, channels).astype(jnp.bfloat16)
        self.east_out[first : first + pairs] = split[:, :, 8:].reshape(pairs, 16, channels).astype(jnp.bfloat16)

    def send_part(self, part):
        lo, hi = self.cuts[part], self.cuts[part + 1]
        self.parts.append([
            self.copy(self.east_out.at[lo:hi], self.west_in.at[lo + 1 : hi + 1], (0, 1)),
            self.copy(self.west_out.at[lo:hi], self.east_in.at[lo + 1 : hi + 1], (0, -1)),
        ])

    def send_north(self):
        rows, last = self.rows, self.pairs + 1
        self.bottom = [
            self.copy(self.own.at[2:4], self.own.at[rows + 2 : rows + 4], (-1, 0)),
            self.copy(self.east_out.at[0:1], self.west_in.at[last : last + 1], (-1, 1)),
            self.copy(self.west_out.at[0:1], self.east_in.at[last : last + 1], (-1, -1)),
        ]

    def send_south(self):
        rows, last = self.rows, self.pairs - 1
        self.top = [
            self.copy(self.own.at[rows : rows + 2], self.own.at[0:2], (1, 0)),
            self.copy(self.east_out.at[last : last + 1], self.west_in.at[0:1], (1, 1)),
            self.copy(self.west_out.at[last : last + 1], self.east_in.at[0:1], (1, -1)),
        ]

    def wait(self, copies):
        for copy in copies:
            copy.wait_recv()

    def window(self, first):
        channels = self.own.shape[-1]
        pair = first // 2
        return jnp.concatenate([
            self.own[first : first + 8].reshape(128, channels),
            self.west_in[pair : pair + 4].reshape(64, channels),
            self.east_in[pair : pair + 4].reshape(64, channels),
        ], axis=0)


def iota(shape, dim):
    return lax.broadcasted_iota(jnp.int32, shape, dim)


def lay_taps(filter_basis, half_widths, stage, taps):
    taps_lat, taps_lon, kernels, rows = filter_basis.shape
    allowed = jnp.abs(iota((taps_lon, rows), 0) - taps_lon // 2) <= half_widths[...].reshape(1, rows)
    stage[...] = jnp.zeros_like(stage)
    taps[...] = jnp.zeros_like(taps)
    for b in range(kernels):
        for s in range(taps_lat):
            values = jnp.where(allowed, filter_basis[s].astype(jnp.float32)[:, b], 0.0)
            stage[s * 32 : s * 32 + taps_lon, 0:rows] = values
        taps[b, 8 : 8 + stage.shape[1]] = stage[...].T


def base_rows(taps, b, first, rows, total_rows, backward):
    reach = 2
    near = taps[b, pl.ds(first, rows + 16)]
    lane = iota((rows, 256), 1)
    if not backward:
        source = iota((rows, 256), 0) + first + lax.div(lane, 32) - reach
        return jnp.where((source >= 0) & (source < total_rows), near[8 : 8 + rows], 0.0)
    chosen = jnp.zeros((rows, 256), jnp.float32)
    for s in range(5):
        start = 8 + reach - s
        chosen = jnp.where(lax.div(lane, 32) == s, near[start : start + rows], chosen)
    turned = (iota((256, 256), 0) + iota((256, 256), 1) == 144).astype(jnp.bfloat16)
    return jnp.dot(chosen.astype(jnp.bfloat16), turned, preferred_element_type=jnp.float32)


def lay_band(taps, base, moved, band, first, rows, total_rows, backward):
    kernels, blocks = taps.shape[0], rows // 4
    for b in range(kernels):
        base[b] = base_rows(taps, b, first, rows, total_rows, backward)

    def move(n, carry):
        for a in range(4):
            for b in range(kernels):
                row = jnp.broadcast_to(base[b, pl.ds(n * 4 + a, 1)], (16, 256))
                moved[a, n, b] = pltpu.roll(row, 0, 1, stride=1, stride_axis=0).astype(jnp.bfloat16)
        return carry

    lax.fori_loop(0, blocks, move, 0)
    place = iota((256, 256), 1)
    west, east = place - 128, place - 192
    own = lax.div(place, 16) * 32 + 8 + lax.rem(place, 16)
    side = jnp.where(place < 192, lax.div(west, 8) * 32 + lax.rem(west, 8), lax.div(east, 8) * 32 + 24 + lax.rem(east, 8))
    wanted = jnp.where(place < 128, own, side)
    for a in range(4):
        table = (iota((256, 256), 0) == wanted - 32 * a).astype(jnp.bfloat16)

        rows_in = moved[a].reshape(blocks * kernels * 16, 256)
        out = jnp.dot(rows_in, table, preferred_element_type=jnp.float32).astype(jnp.bfloat16)
        band[:, :, a] = out.reshape(blocks, kernels, 16, 256)


def gelu_slope(values):
    cdf = 0.5 * (1.0 + lax.erf(values * math.sqrt(0.5)))
    return cdf + values * (jnp.exp(values * values * -0.5) * (1.0 / math.sqrt(2.0 * math.pi)))


def apply_blocks(band, halo, flat, part, channels, blocks):
    for n in range(part * blocks, (part + 1) * blocks):
        out = jnp.dot(band[n].reshape(192, 256), halo.window(n * 4), preferred_element_type=jnp.float32).astype(jnp.bfloat16)
        for b in range(3):
            flat[n * 64 : (n + 1) * 64, b * channels : (b + 1) * channels] = out[b * 64 : (b + 1) * 64]


def block_kernel(
    scale, features_hbm, filter_hbm, half_widths, mixing_hbm, bias, cotangent_hbm, grad_hbm, mixing_out,
    own, west_in, east_in, west_out, east_out, send, recv,
    g_own, g_west_in, g_east_in, g_west_out, g_east_out, g_send, g_recv,
    mixing, cotangent, result, flat, local, stage, taps, base, moved, band, g_band, filter_basis, load_sem, store_sem, *sum_refs):
    rows, width, channels = cotangent.shape
    kernels, total_rows = filter_basis.shape[2:]
    parts, part_rows = 5, rows // 5
    blocks = part_rows // 4
    pairs = part_rows // 2
    loads = [
        pltpu.make_async_copy(features_hbm, own.at[2 : rows + 2], load_sem.at[0]),
        pltpu.make_async_copy(filter_hbm, filter_basis, load_sem.at[3]),
        pltpu.make_async_copy(mixing_hbm, mixing, load_sem.at[1]),
        pltpu.make_async_copy(cotangent_hbm, cotangent, load_sem.at[2]),
    ]
    for load in loads:
        load.start()
    peers = list(halo_peers().values()) + sum_peers()
    greet(peers)
    work = SumOverAll(mixing.shape[0] // (2 * SIZE_X), channels, sum_refs, scale)
    cuts = [0] + [pairs * part + 1 for part in range(1, parts)] + [rows // 2]
    halo = Halo(own, west_in, east_in, west_out, east_out, send, recv, cuts)
    g_halo = Halo(g_own, g_west_in, g_east_in, g_west_out, g_east_out, g_send, g_recv, [pairs * part for part in range(parts + 1)])
    loads[0].wait()
    for part in range(parts):
        lo, hi = cuts[part], cuts[part + 1]
        halo.pack(lo, own[2 + 2 * lo : 2 + 2 * hi].astype(jnp.float32))
    work.clear()
    await_greetings(len(peers))
    halo.send_north()
    halo.send_south()
    halo.send_part(0)
    halo.send_part(1)

    first = pl.multiple_of(lax.axis_index("lat") * rows, 8)
    loads[1].wait()
    lay_taps(filter_basis, half_widths, stage, taps)
    lay_band(taps, base, moved, band, first, rows, total_rows, False)
    for part in (0, 1):
        halo.left(part)
        halo.send_part(part + 2)
    loads[2].wait()
    loads[3].wait()
    halo.wait(halo.top)
    cells = part_rows * width
    for part in range(parts):
        halo.wait(halo.parts[part])
        if part == 1:
            halo.left(2)
            halo.send_part(4)
        if part == parts - 1:
            halo.left(4)
            for packed in range(part):
                g_halo.send_part(packed)
            g_halo.send_north()
        if part == parts - 1:
            halo.wait(halo.bottom)
        apply_blocks(band, halo, flat, part, channels, blocks)
        here = flat[part * cells : (part + 1) * cells]
        pre = jnp.dot(here, mixing[...], preferred_element_type=jnp.float32) + bias[...].reshape(1, channels)
        at = part * part_rows
        cot = cotangent[at : at + part_rows].reshape(cells, channels).astype(jnp.float32)
        grad = cot * gelu_slope(pre)
        grad_rows = grad.reshape(part_rows, width, channels)
        grad = grad.astype(jnp.bfloat16)
        g_own[2 + at : 2 + at + part_rows] = grad.reshape(part_rows, width, channels)
        g_halo.pack(at // 2, grad_rows)
        if part == parts - 1:
            g_halo.send_part(part)
            g_halo.send_south()
        outer = lax.dot_general(here, grad, (((0,), (0,)), ((), ())), preferred_element_type=jnp.float32)
        if part == 0:
            local[...] = outer
        elif part < parts - 1:
            local[...] += outer
        else:
            work.lay(outer, local)

    work.start_core()
    work.core_to_x()
    lay_band(taps, base, moved, g_band, first, rows, total_rows, True)
    work.x_to_y()
    work.y_to_z()
    steps = {3: work.z_to_gather, 4: work.gather_y}
    stores = []
    g_halo.wait(g_halo.top)
    g_halo.wait(g_halo.parts[0])
    for part in range(parts):
        if part in steps:
            steps[part]()
        if part < parts - 1:
            g_halo.wait(g_halo.parts[part + 1])
        else:
            g_halo.wait(g_halo.bottom)
        apply_blocks(g_band, g_halo, flat, part, channels, blocks)
        here = flat[part * cells : (part + 1) * cells]
        at = part * part_rows
        branch = cotangent[at : at + part_rows].reshape(cells, channels).astype(jnp.float32)
        for b in range(kernels):
            mix = mixing[b * channels : (b + 1) * channels]
            branch = branch + lax.dot_general(
                here[:, b * channels : (b + 1) * channels], mix, (((1,), (1,)), ((), ())), preferred_element_type=jnp.float32)
        result[at : at + part_rows] = branch.astype(jnp.bfloat16).reshape(part_rows, width, channels)
        stores.append(pltpu.make_async_copy(
            result.at[at : at + part_rows], grad_hbm.at[at : at + part_rows], store_sem.at[part]))
        stores[-1].start()
    work.gather_x()
    work.finish(mixing_out)
    for store in stores:
        store.wait()
    halo.drain()
    g_halo.drain()


def halo_buffers(rows, channels, parts):
    side = pltpu.VMEM((rows // 2 + 2, 16, channels), jnp.bfloat16)
    out = pltpu.VMEM((rows // 2, 16, channels), jnp.bfloat16)
    copies = 2 * parts + 6
    return [
        pltpu.VMEM((rows + 4, 16, channels), jnp.bfloat16), side, side, out, out,
        pltpu.SemaphoreType.DMA((copies,)), pltpu.SemaphoreType.DMA((copies,)),
    ]


def per_device(features, filter_basis, half_widths, mixing, channel_bias, cotangent):
    rows, width, channels = features.shape
    kernels, taps_lat, taps_lon, total_rows = filter_basis.shape
    cells = rows * width
    cell_count = cells * lax.axis_size("lat") * lax.axis_size("lon")
    blocks = rows // 4
    lanes = -(-total_rows // 128) * 128
    anywhere, vmem = pl.BlockSpec(memory_space=pltpu.HBM), pl.BlockSpec(memory_space=pltpu.VMEM)
    band = pltpu.VMEM((blocks, kernels, 4, 16, 256), jnp.bfloat16)
    return pl.pallas_call(
        lambda *refs: block_kernel(math.sqrt(cell_count), *refs),
        out_shape=(
            jax.ShapeDtypeStruct((rows, width, channels), jnp.bfloat16),
            jax.ShapeDtypeStruct((kernels * channels, channels), jnp.bfloat16),
        ),
        in_specs=[anywhere, anywhere, vmem, anywhere, vmem, anywhere],
        out_specs=(anywhere, vmem),
        scratch_shapes=[
            *halo_buffers(rows, channels, 5),
            *halo_buffers(rows, channels, 5),
            pltpu.VMEM((kernels * channels, channels), jnp.bfloat16),
            pltpu.VMEM((rows, width, channels), jnp.bfloat16),
            pltpu.VMEM((rows, width, channels), jnp.bfloat16),
            pltpu.VMEM((cells, kernels * channels), jnp.bfloat16),
            pltpu.VMEM((kernels * channels, channels), jnp.float32),
            pltpu.VMEM((256, lanes), jnp.float32),
            pltpu.VMEM((kernels, lanes + 16, 256), jnp.float32),
            pltpu.VMEM((kernels, rows, 256), jnp.float32),
            pltpu.VMEM((4, blocks, kernels, 16, 256), jnp.bfloat16),
            band,
            band,
            pltpu.VMEM((taps_lat, taps_lon, kernels, total_rows), jnp.bfloat16),
            pltpu.SemaphoreType.DMA((4,)),
            pltpu.SemaphoreType.DMA((5,)),
            *sum_buffers(),
        ],
        compiler_params=pltpu.CompilerParams(
            collective_id=0, has_side_effects=True, vmem_limit_bytes=56 * 1024 * 1024),
    )(features, filter_basis.transpose(1, 2, 0, 3), half_widths, mixing, channel_bias, cotangent)


def solution(mesh):
    return jax.shard_map(
        per_device,
        mesh=mesh,
        in_specs=(P("lat", "lon", None), P(), P(), P(), P(), P("lat", "lon", None)),
        out_specs=(P("lat", "lon", None), P()),
        check_vma=False,
    )
```

```python
import math

import jax
import jax.numpy as jnp
from jax import lax
from jax.experimental import pallas as pl
from jax.experimental.pallas import tpu as pltpu
from jax.sharding import PartitionSpec as P

MESH = pl.DeviceIdType.MESH
SIZE_X_LO, SIZE_Z, SIZE_Y = 2, 8, 8
SIZE_X = 4


def position():
    lon, lat = lax.axis_index("lon"), lax.axis_index("lat")
    x = lax.div(lat, 2) * SIZE_X_LO + lax.div(lon, SIZE_Z * SIZE_Y)
    z = lax.rem(lax.div(lon, SIZE_Y), SIZE_Z)
    return x, z, lax.rem(lon, SIZE_Y), lax.rem(lat, 2)


def device(x, z, y, core):
    lon = (lax.rem(x, SIZE_X_LO) * SIZE_Z + z) * SIZE_Y + y
    return {"lon": lon, "lat": lax.div(x, SIZE_X_LO) * 2 + core}


def sum_peers():
    x, z, y, core = position()
    peers = [device(x, z, y, 1 - core)]
    peers += [device(lax.rem(x + d, SIZE_X), z, y, core) for d in range(1, SIZE_X)]
    peers += [device(x, lax.rem(z + d, SIZE_Z), y, core) for d in range(1, SIZE_Z)]
    peers += [device(x, z, lax.rem(y + d, SIZE_Y), core) for d in range(1, SIZE_Y)]
    return peers


def greet(peers):
    barrier = pltpu.get_barrier_semaphore()
    for peer in peers:
        pl.semaphore_signal(barrier, inc=1, device_id=peer, device_id_type=MESH)


def await_greetings(count):
    pl.semaphore_wait(pltpu.get_barrier_semaphore(), count)


SHARE = 4
Y_ORDER = (4, 3, 5, 2, 6, 1, 7, 0)
GATHER_ORDER = (0, 1, 7, 2, 6, 3, 5, 4)


def tile_count(part_rows, channels):
    tiles = (part_rows // 16) * (channels // 128)
    assert (SIZE_Y - 1) * SHARE <= tiles + 1 <= SIZE_Y * SHARE
    return tiles


def sum_buffers():
    pieces = (SIZE_Y, SIZE_X, SHARE, 16, 128)
    copies = SIZE_Y + 2 * SIZE_Y * (SIZE_X - 1) + 2 * (SIZE_Y - 1) + SIZE_Z - 1 + SIZE_X
    return [
        pltpu.VMEM((2, *pieces), jnp.float32),
        pltpu.VMEM(pieces, jnp.float32),
        pltpu.VMEM(pieces, jnp.bfloat16),
        pltpu.VMEM((SIZE_X - 1, SIZE_Y, SHARE, 16, 128), jnp.bfloat16),
        pltpu.VMEM((SIZE_Y - 1, SHARE, 16, 128), jnp.bfloat16),
        pltpu.VMEM((SIZE_Y - 1, SHARE, 16, 128), jnp.bfloat16),
        pltpu.VMEM((SIZE_Z, SHARE, 16, 128), jnp.bfloat16),
        pltpu.VMEM((2, SIZE_X, SIZE_Y, SHARE, 16, 128), jnp.bfloat16),
        pltpu.SemaphoreType.DMA((copies,)),
        pltpu.SemaphoreType.DMA((copies,)),
    ]


class SumOverAll:
    def __init__(self, rows, channels, buffers, scale):
        (self.local, self.half, self.x_out, self.x_in, self.y_out, self.y_in, self.z_all, self.done, self.send, self.recv) = buffers
        self.rows, self.lanes, self.tiles, self.scale = rows, channels // 128, tile_count(rows, channels), scale
        self.x, self.z, self.y, self.core = position()
        self.used, self.sent = 0, []

    def copy(self, src, dst, peer):
        index = self.used
        self.used += 1
        copy = pltpu.make_async_remote_copy(
            src_ref=src, dst_ref=dst, send_sem=self.send.at[index], recv_sem=self.recv.at[index],
            device_id=peer, device_id_type=MESH)
        copy.start()
        self.sent.append(copy)
        return copy

    def other_core(self):
        return device(self.x, self.z, self.y, 1 - self.core)

    def other_x(self, d):
        return device(lax.rem(self.x + d, SIZE_X), self.z, self.y, self.core)

    def other_y(self, d):
        return device(self.x, self.z, lax.rem(self.y + d, SIZE_Y), self.core)

    def other_z(self, d):
        return device(self.x, lax.rem(self.z + d, SIZE_Z), self.y, self.core)

    def places(self, core, part):
        for t in range(self.tiles):
            row = (core * SIZE_X + part) * self.rows + t // self.lanes * 16
            lane = t % self.lanes * 128
            yield t // SHARE, t % SHARE, slice(row, row + 16), slice(lane, lane + 128)

    def clear(self):
        self.local[:, SIZE_Y - 2 :] = jnp.zeros_like(self.local[:, SIZE_Y - 2 :])

    def lay(self, values, more):
        for core in range(2):
            for part in range(SIZE_X):
                for y, slot, rows, lanes in self.places(core, part):
                    self.local[core, y, part, slot] = values[rows, lanes] + more[rows, lanes]

    def start_core(self):
        self.from_core = {}
        for d in Y_ORDER:
            y = lax.rem(self.y + d, SIZE_Y)
            self.from_core[d] = self.copy(self.local.at[1 - self.core, y], self.half.at[y], self.other_core())

    def core_to_x(self):
        self.from_x = {}
        for d in Y_ORDER:
            y = lax.rem(self.y + d, SIZE_Y)
            self.from_core[d].wait_recv()
            total = self.half[y] + self.local[self.core, y]
            self.half[y] = total
            self.x_out[y] = total.astype(jnp.bfloat16)
            self.from_x[d] = [
                self.copy(self.x_out.at[y, lax.rem(self.x + e, SIZE_X)], self.x_in.at[e - 1, y], self.other_x(e))
                for e in (2, 1, 3)
            ]

    def x_to_y(self):
        self.from_y = []
        for d in Y_ORDER:
            y = lax.rem(self.y + d, SIZE_Y)
            total = self.half[y, self.x]
            for copy in self.from_x[d]:
                copy.wait_recv()
            for e in range(SIZE_X - 1):
                total = total + self.x_in[e, y].astype(jnp.float32)
            if d:
                self.y_out[d - 1] = total.astype(jnp.bfloat16)
                self.from_y.append(self.copy(self.y_out.at[d - 1], self.y_in.at[d - 1], self.other_y(d)))
            else:
                self.half[y, self.x] = total

    def y_to_z(self):
        total = self.half[self.y, self.x]
        for copy in self.from_y:
            copy.wait_recv()
        for d in range(SIZE_Y - 1):
            total = total + self.y_in[d].astype(jnp.float32)
        self.z_all[self.z] = total.astype(jnp.bfloat16)
        piece = self.z_all.at[self.z]
        self.from_z = [self.copy(piece, piece, self.other_z(d)) for d in (4, 3, 5, 2, 6, 1, 7)]

    def spread_x(self, d):
        y = lax.rem(self.y + SIZE_Y - d, SIZE_Y)
        piece = self.done.at[self.core, self.x, y]
        for e in (2, 1, 3):
            self.gathered[e].append(self.copy(piece, piece, self.other_x(e)))

    def z_to_gather(self):
        for copy in self.from_z:
            copy.wait_recv()
        total = self.z_all[0].astype(jnp.float32)
        for other in range(1, SIZE_Z):
            total = total + self.z_all[other].astype(jnp.float32)
        self.done[self.core, self.x, self.y] = (total / self.scale).astype(jnp.bfloat16)
        piece = self.done.at[self.core, self.x, self.y]
        self.y_gathered = {d: self.copy(piece, piece, self.other_y(d)) for d in (4, 3, 5, 2, 6, 1, 7)}
        self.gathered = {e: [] for e in range(1, SIZE_X)}
        self.spread_x(0)

    def gather_y(self):
        for d in GATHER_ORDER[1:]:
            self.y_gathered[d].wait_recv()
            self.spread_x(d)
        self.spread_core(0)

    def spread_core(self, e):
        part = self.done.at[self.core, lax.rem(self.x + SIZE_X - e, SIZE_X)]
        self.copy(part, part, self.other_core())

    def gather_x(self):
        for e in (1, 3, 2):
            for copy in self.gathered[e]:
                copy.wait_recv()
            self.spread_core(e)

    def finish(self, out):
        for copy in self.sent[-SIZE_X:]:
            copy.wait_recv()
        for core in range(2):
            for part in range(SIZE_X):
                for y, slot, rows, lanes in self.places(core, part):
                    out[rows, lanes] = self.done[core, part, y, slot]
        for copy in self.sent:
            copy.wait_send()


def halo_peers():
    lon, lat = lax.axis_index("lon"), lax.axis_index("lat")
    count_lon, count_lat = lax.axis_size("lon"), lax.axis_size("lat")
    east, west = lax.rem(lon + 1, count_lon), lax.rem(lon + count_lon - 1, count_lon)
    south, north = lax.rem(lat + 1, count_lat), lax.rem(lat + count_lat - 1, count_lat)
    return {
        (row, column): {"lon": at_lon, "lat": at_lat}
        for row, at_lat in ((-1, north), (0, lat), (1, south))
        for column, at_lon in ((-1, west), (0, lon), (1, east))
        if (row, column) != (0, 0)
    }


class Halo:
    def __init__(self, own, west_in, east_in, west_out, east_out, send, recv, cuts):
        self.own, self.west_in, self.east_in = own, west_in, east_in
        self.west_out, self.east_out, self.send, self.recv = west_out, east_out, send, recv
        self.peers, self.rows, self.cuts, self.used = halo_peers(), own.shape[0] - 4, cuts, 0
        self.pairs, self.parts, self.top, self.bottom, self.sent = self.rows // 2, [], [], [], []

    def copy(self, src, dst, peer):
        index = self.used
        self.used += 1
        copy = pltpu.make_async_remote_copy(
            src_ref=src, dst_ref=dst, send_sem=self.send.at[index], recv_sem=self.recv.at[index],
            device_id=self.peers[peer], device_id_type=MESH)
        copy.start()
        self.sent.append(copy)
        return copy

    def left(self, part):
        for copy in self.parts[part]:
            copy.wait_send()
            self.sent = [other for other in self.sent if other is not copy]

    def drain(self):
        for copy in self.sent:
            copy.wait_send()

    def pack(self, first, values):
        pairs, channels = values.shape[0] // 2, values.shape[-1]
        split = values.reshape(pairs, 2, 16, channels)
        self.west_out[first : first + pairs] = split[:, :, :8].reshape(pairs, 16, channels).astype(jnp.bfloat16)
        self.east_out[first : first + pairs] = split[:, :, 8:].reshape(pairs, 16, channels).astype(jnp.bfloat16)

    def send_part(self, part):
        lo, hi = self.cuts[part], self.cuts[part + 1]
        self.parts.append([
            self.copy(self.east_out.at[lo:hi], self.west_in.at[lo + 1 : hi + 1], (0, 1)),
            self.copy(self.west_out.at[lo:hi], self.east_in.at[lo + 1 : hi + 1], (0, -1)),
        ])

    def send_north(self):
        rows, last = self.rows, self.pairs + 1
        self.bottom = [
            self.copy(self.own.at[2:4], self.own.at[rows + 2 : rows + 4], (-1, 0)),
            self.copy(self.east_out.at[0:1], self.west_in.at[last : last + 1], (-1, 1)),
            self.copy(self.west_out.at[0:1], self.east_in.at[last : last + 1], (-1, -1)),
        ]

    def send_south(self):
        rows, last = self.rows, self.pairs - 1
        self.top = [
            self.copy(self.own.at[rows : rows + 2], self.own.at[0:2], (1, 0)),
            self.copy(self.east_out.at[last : last + 1], self.west_in.at[0:1], (1, 1)),
            self.copy(self.west_out.at[last : last + 1], self.east_in.at[0:1], (1, -1)),
        ]

    def wait(self, copies):
        for copy in copies:
            copy.wait_recv()

    def window(self, first):
        channels = self.own.shape[-1]
        pair = first // 2
        return jnp.concatenate([
            self.own[first : first + 8].reshape(128, channels),
            self.west_in[pair : pair + 4].reshape(64, channels),
            self.east_in[pair : pair + 4].reshape(64, channels),
        ], axis=0)


def iota(shape, dim):
    return lax.broadcasted_iota(jnp.int32, shape, dim)


def lay_taps(filter_basis, half_widths, stage, taps):
    taps_lat, taps_lon, kernels, rows = filter_basis.shape
    allowed = jnp.abs(iota((taps_lon, rows), 0) - taps_lon // 2) <= half_widths[...].reshape(1, rows)
    stage[...] = jnp.zeros_like(stage)
    taps[...] = jnp.zeros_like(taps)
    for b in range(kernels):
        for s in range(taps_lat):
            values = jnp.where(allowed, filter_basis[s].astype(jnp.float32)[:, b], 0.0)
            stage[s * 32 : s * 32 + taps_lon, 0:rows] = values
        taps[b, 8 : 8 + stage.shape[1]] = stage[...].T


def base_rows(taps, b, first, rows, total_rows, backward):
    reach = 2
    near = taps[b, pl.ds(first, rows + 16)]
    lane = iota((rows, 256), 1)
    if not backward:
        source = iota((rows, 256), 0) + first + lax.div(lane, 32) - reach
        return jnp.where((source >= 0) & (source < total_rows), near[8 : 8 + rows], 0.0)
    chosen = jnp.zeros((rows, 256), jnp.float32)
    for s in range(5):
        start = 8 + reach - s
        chosen = jnp.where(lax.div(lane, 32) == s, near[start : start + rows], chosen)
    turned = (iota((256, 256), 0) + iota((256, 256), 1) == 144).astype(jnp.bfloat16)
    return jnp.dot(chosen.astype(jnp.bfloat16), turned, preferred_element_type=jnp.float32)


def lay_band(taps, base, moved, band, first, rows, total_rows, backward):
    kernels, blocks = taps.shape[0], rows // 4
    for b in range(kernels):
        base[b] = base_rows(taps, b, first, rows, total_rows, backward)

    def move(n, carry):
        for a in range(4):
            for b in range(kernels):
                row = jnp.broadcast_to(base[b, pl.ds(n * 4 + a, 1)], (16, 256))
                moved[a, n, b] = pltpu.roll(row, 0, 1, stride=1, stride_axis=0).astype(jnp.bfloat16)
        return carry

    lax.fori_loop(0, blocks, move, 0)
    place = iota((256, 256), 1)
    west, east = place - 128, place - 192
    own = lax.div(place, 16) * 32 + 8 + lax.rem(place, 16)
    side = jnp.where(place < 192, lax.div(west, 8) * 32 + lax.rem(west, 8), lax.div(east, 8) * 32 + 24 + lax.rem(east, 8))
    wanted = jnp.where(place < 128, own, side)
    for a in range(4):
        table = (iota((256, 256), 0) == wanted - 32 * a).astype(jnp.bfloat16)

        rows_in = moved[a].reshape(blocks * kernels * 16, 256)
        out = jnp.dot(rows_in, table, preferred_element_type=jnp.float32).astype(jnp.bfloat16)
        band[:, :, a] = out.reshape(blocks, kernels, 16, 256)


def gelu_slope(values):
    cdf = 0.5 * (1.0 + lax.erf(values * math.sqrt(0.5)))
    return cdf + values * (jnp.exp(values * values * -0.5) * (1.0 / math.sqrt(2.0 * math.pi)))


def apply_blocks(band, halo, flat, part, channels, blocks):
    for n in range(part * blocks, (part + 1) * blocks):
        out = jnp.dot(band[n].reshape(192, 256), halo.window(n * 4), preferred_element_type=jnp.float32).astype(jnp.bfloat16)
        for b in range(3):
            flat[n * 64 : (n + 1) * 64, b * channels : (b + 1) * channels] = out[b * 64 : (b + 1) * 64]


def block_kernel(
    scale, features_hbm, filter_hbm, half_widths, mixing_hbm, bias, cotangent_hbm, grad_hbm, mixing_out,
    own, west_in, east_in, west_out, east_out, send, recv,
    g_own, g_west_in, g_east_in, g_west_out, g_east_out, g_send, g_recv,
    mixing, cotangent, result, flat, local, stage, taps, base, moved, band, g_band, filter_basis, load_sem, store_sem, *sum_refs):
    rows, width, channels = cotangent.shape
    kernels, total_rows = filter_basis.shape[2:]
    parts, part_rows = 5, rows // 5
    blocks = part_rows // 4
    pairs = part_rows // 2
    loads = [
        pltpu.make_async_copy(features_hbm, own.at[2 : rows + 2], load_sem.at[0]),
        pltpu.make_async_copy(filter_hbm, filter_basis, load_sem.at[3]),
        pltpu.make_async_copy(mixing_hbm, mixing, load_sem.at[1]),
        pltpu.make_async_copy(cotangent_hbm, cotangent, load_sem.at[2]),
    ]
    for load in loads:
        load.start()
    peers = list(halo_peers().values()) + sum_peers()
    greet(peers)
    work = SumOverAll(mixing.shape[0] // (2 * SIZE_X), channels, sum_refs, scale)
    cuts = [0] + [pairs * part + 1 for part in range(1, parts)] + [rows // 2]
    halo = Halo(own, west_in, east_in, west_out, east_out, send, recv, cuts)
    g_halo = Halo(g_own, g_west_in, g_east_in, g_west_out, g_east_out, g_send, g_recv, [pairs * part for part in range(parts + 1)])
    loads[0].wait()
    for part in range(parts):
        lo, hi = cuts[part], cuts[part + 1]
        halo.pack(lo, own[2 + 2 * lo : 2 + 2 * hi].astype(jnp.float32))
    work.clear()
    await_greetings(len(peers))
    halo.send_north()
    halo.send_south()
    halo.send_part(0)
    halo.send_part(1)

    first = pl.multiple_of(lax.axis_index("lat") * rows, 8)
    loads[1].wait()
    lay_taps(filter_basis, half_widths, stage, taps)
    lay_band(taps, base, moved, band, first, rows, total_rows, False)
    for part in (0, 1):
        halo.left(part)
        halo.send_part(part + 2)
    loads[2].wait()
    loads[3].wait()
    halo.wait(halo.top)
    cells = part_rows * width
    for part in range(parts):
        halo.wait(halo.parts[part])
        if part == 1:
            halo.left(2)
            halo.send_part(4)
        if part == parts - 1:
            halo.wait(halo.bottom)
        apply_blocks(band, halo, flat, part, channels, blocks)
        here = flat[part * cells : (part + 1) * cells]
        pre = jnp.dot(here, mixing[...], preferred_element_type=jnp.float32) + bias[...].reshape(1, channels)
        at = part * part_rows
        cot = cotangent[at : at + part_rows].reshape(cells, channels).astype(jnp.float32)
        grad = cot * gelu_slope(pre)
        grad_rows = grad.reshape(part_rows, width, channels)
        grad = grad.astype(jnp.bfloat16)
        g_own[2 + at : 2 + at + part_rows] = grad.reshape(part_rows, width, channels)
        g_halo.pack(at // 2, grad_rows)
        g_halo.send_part(part)
        if part == 0:
            g_halo.send_north()
        if part == parts - 1:
            g_halo.send_south()
        outer = lax.dot_general(here, grad, (((0,), (0,)), ((), ())), preferred_element_type=jnp.float32)
        if part == 0:
            local[...] = outer
        elif part < parts - 1:
            local[...] += outer
        else:
            work.lay(outer, local)

    work.start_core()
    work.core_to_x()
    lay_band(taps, base, moved, g_band, first, rows, total_rows, True)
    work.x_to_y()
    work.y_to_z()
    steps = {2: work.z_to_gather, 3: work.gather_y}
    stores = []
    g_halo.wait(g_halo.top)
    g_halo.wait(g_halo.parts[0])
    for part in range(parts):
        if part in steps:
            steps[part]()
        if part < parts - 1:
            g_halo.wait(g_halo.parts[part + 1])
        else:
            g_halo.wait(g_halo.bottom)
        apply_blocks(g_band, g_halo, flat, part, channels, blocks)
        here = flat[part * cells : (part + 1) * cells]
        at = part * part_rows
        branch = cotangent[at : at + part_rows].reshape(cells, channels).astype(jnp.float32)
        for b in range(kernels):
            mix = mixing[b * channels : (b + 1) * channels]
            branch = branch + lax.dot_general(
                here[:, b * channels : (b + 1) * channels], mix, (((1,), (1,)), ((), ())), preferred_element_type=jnp.float32)
        result[at : at + part_rows] = branch.astype(jnp.bfloat16).reshape(part_rows, width, channels)
        stores.append(pltpu.make_async_copy(
            result.at[at : at + part_rows], grad_hbm.at[at : at + part_rows], store_sem.at[part]))
        stores[-1].start()
    work.gather_x()
    work.finish(mixing_out)
    for store in stores:
        store.wait()
    halo.drain()
    g_halo.drain()


def halo_buffers(rows, channels, parts):
    side = pltpu.VMEM((rows // 2 + 2, 16, channels), jnp.bfloat16)
    out = pltpu.VMEM((rows // 2, 16, channels), jnp.bfloat16)
    copies = 2 * parts + 6
    return [
        pltpu.VMEM((rows + 4, 16, channels), jnp.bfloat16), side, side, out, out,
        pltpu.SemaphoreType.DMA((copies,)), pltpu.SemaphoreType.DMA((copies,)),
    ]


def per_device(features, filter_basis, half_widths, mixing, channel_bias, cotangent):
    rows, width, channels = features.shape
    kernels, taps_lat, taps_lon, total_rows = filter_basis.shape
    cells = rows * width
    cell_count = cells * lax.axis_size("lat") * lax.axis_size("lon")
    blocks = rows // 4
    lanes = -(-total_rows // 128) * 128
    anywhere, vmem = pl.BlockSpec(memory_space=pltpu.HBM), pl.BlockSpec(memory_space=pltpu.VMEM)
    band = pltpu.VMEM((blocks, kernels, 4, 16, 256), jnp.bfloat16)
    return pl.pallas_call(
        lambda *refs: block_kernel(math.sqrt(cell_count), *refs),
        out_shape=(
            jax.ShapeDtypeStruct((rows, width, channels), jnp.bfloat16),
            jax.ShapeDtypeStruct((kernels * channels, channels), jnp.bfloat16),
        ),
        in_specs=[anywhere, anywhere, vmem, anywhere, vmem, anywhere],
        out_specs=(anywhere, vmem),
        scratch_shapes=[
            *halo_buffers(rows, channels, 5),
            *halo_buffers(rows, channels, 5),
            pltpu.VMEM((kernels * channels, channels), jnp.bfloat16),
            pltpu.VMEM((rows, width, channels), jnp.bfloat16),
            pltpu.VMEM((rows, width, channels), jnp.bfloat16),
            pltpu.VMEM((cells, kernels * channels), jnp.bfloat16),
            pltpu.VMEM((kernels * channels, channels), jnp.float32),
            pltpu.VMEM((256, lanes), jnp.float32),
            pltpu.VMEM((kernels, lanes + 16, 256), jnp.float32),
            pltpu.VMEM((kernels, rows, 256), jnp.float32),
            pltpu.VMEM((4, blocks, kernels, 16, 256), jnp.bfloat16),
            band,
            band,
            pltpu.VMEM((taps_lat, taps_lon, kernels, total_rows), jnp.bfloat16),
            pltpu.SemaphoreType.DMA((4,)),
            pltpu.SemaphoreType.DMA((5,)),
            *sum_buffers(),
        ],
        compiler_params=pltpu.CompilerParams(
            collective_id=0, has_side_effects=True, vmem_limit_bytes=56 * 1024 * 1024),
    )(features, filter_basis.transpose(1, 2, 0, 3), half_widths, mixing, channel_bias, cotangent)


def solution(mesh):
    return jax.shard_map(
        per_device,
        mesh=mesh,
        in_specs=(P("lat", "lon", None), P(), P(), P(), P(), P("lat", "lon", None)),
        out_specs=(P("lat", "lon", None), P()),
        check_vma=False,
    )
```

```python
import math

import jax
import jax.numpy as jnp
from jax import lax
from jax.experimental import pallas as pl
from jax.experimental.pallas import tpu as pltpu
from jax.sharding import PartitionSpec as P

MESH = pl.DeviceIdType.MESH
SIZE_X_LO, SIZE_Z, SIZE_Y = 2, 8, 8
SIZE_X = 4


def position():
    lon, lat = lax.axis_index("lon"), lax.axis_index("lat")
    x = lax.div(lat, 2) * SIZE_X_LO + lax.div(lon, SIZE_Z * SIZE_Y)
    z = lax.rem(lax.div(lon, SIZE_Y), SIZE_Z)
    return x, z, lax.rem(lon, SIZE_Y), lax.rem(lat, 2)


def device(x, z, y, core):
    lon = (lax.rem(x, SIZE_X_LO) * SIZE_Z + z) * SIZE_Y + y
    return {"lon": lon, "lat": lax.div(x, SIZE_X_LO) * 2 + core}


def sum_peers():
    x, z, y, core = position()
    peers = [device(x, z, y, 1 - core)]
    peers += [device(lax.rem(x + d, SIZE_X), z, y, core) for d in range(1, SIZE_X)]
    peers += [device(x, lax.rem(z + d, SIZE_Z), y, core) for d in range(1, SIZE_Z)]
    peers += [device(x, z, lax.rem(y + d, SIZE_Y), core) for d in range(1, SIZE_Y)]
    return peers


def greet(peers):
    barrier = pltpu.get_barrier_semaphore()
    for peer in peers:
        pl.semaphore_signal(barrier, inc=1, device_id=peer, device_id_type=MESH)


def await_greetings(count):
    pl.semaphore_wait(pltpu.get_barrier_semaphore(), count)


SHARE = 4
Y_ORDER = (4, 3, 5, 2, 6, 1, 7, 0)
GATHER_ORDER = (0, 1, 7, 2, 6, 3, 5, 4)


def tile_count(part_rows, channels):
    tiles = (part_rows // 16) * (channels // 128)
    assert (SIZE_Y - 1) * SHARE <= tiles + 1 <= SIZE_Y * SHARE
    return tiles


def sum_buffers():
    pieces = (SIZE_Y, SIZE_X, SHARE, 16, 128)
    copies = SIZE_Y + 2 * SIZE_Y * (SIZE_X - 1) + 2 * (SIZE_Y - 1) + SIZE_Z - 1 + SIZE_X
    return [
        pltpu.VMEM((2, *pieces), jnp.float32),
        pltpu.VMEM(pieces, jnp.float32),
        pltpu.VMEM(pieces, jnp.bfloat16),
        pltpu.VMEM((SIZE_X - 1, SIZE_Y, SHARE, 16, 128), jnp.bfloat16),
        pltpu.VMEM((SIZE_Y - 1, SHARE, 16, 128), jnp.bfloat16),
        pltpu.VMEM((SIZE_Y - 1, SHARE, 16, 128), jnp.bfloat16),
        pltpu.VMEM((SIZE_Z, SHARE, 16, 128), jnp.bfloat16),
        pltpu.VMEM((2, SIZE_X, SIZE_Y, SHARE, 16, 128), jnp.bfloat16),
        pltpu.SemaphoreType.DMA((copies,)),
        pltpu.SemaphoreType.DMA((copies,)),
    ]


class SumOverAll:
    def __init__(self, rows, channels, buffers, scale):
        (self.local, self.half, self.x_out, self.x_in, self.y_out, self.y_in, self.z_all, self.done, self.send, self.recv) = buffers
        self.rows, self.lanes, self.tiles, self.scale = rows, channels // 128, tile_count(rows, channels), scale
        self.x, self.z, self.y, self.core = position()
        self.used, self.sent = 0, []
        self.mine = self.has(self.y)

    def has(self, y):
        return y < SIZE_Y - 1

    def copy(self, when, src, dst, peer):
        index = self.used
        self.used += 1
        copy = pltpu.make_async_remote_copy(
            src_ref=src, dst_ref=dst, send_sem=self.send.at[index], recv_sem=self.recv.at[index],
            device_id=peer, device_id_type=MESH)
        pl.when(when)(copy.start)
        self.sent.append((when, copy))
        return copy

    def other_core(self):
        return device(self.x, self.z, self.y, 1 - self.core)

    def other_x(self, d):
        return device(lax.rem(self.x + d, SIZE_X), self.z, self.y, self.core)

    def other_y(self, d):
        return device(self.x, self.z, lax.rem(self.y + d, SIZE_Y), self.core)

    def other_z(self, d):
        return device(self.x, lax.rem(self.z + d, SIZE_Z), self.y, self.core)

    def places(self, core, part):
        for t in range(self.tiles):
            row = (core * SIZE_X + part) * self.rows + t // self.lanes * 16
            lane = t % self.lanes * 128
            yield t // SHARE, t % SHARE, slice(row, row + 16), slice(lane, lane + 128)

    def clear(self):
        self.local[:, SIZE_Y - 2 :] = jnp.zeros_like(self.local[:, SIZE_Y - 2 :])

    def lay(self, values, more):
        for core in range(2):
            for part in range(SIZE_X):
                for y, slot, rows, lanes in self.places(core, part):
                    self.local[core, y, part, slot] = values[rows, lanes] + more[rows, lanes]

    def start_core(self):
        self.from_core = {}
        for d in Y_ORDER:
            y = lax.rem(self.y + d, SIZE_Y)
            self.from_core[d] = self.copy(self.has(y), self.local.at[1 - self.core, y], self.half.at[y], self.other_core())

    def core_to_x(self):
        self.from_x = {}
        for d in Y_ORDER:
            y = lax.rem(self.y + d, SIZE_Y)

            @pl.when(self.has(y))
            def _(d=d, y=y):
                self.from_core[d].wait_recv()
                total = self.half[y] + self.local[self.core, y]
                self.half[y] = total
                self.x_out[y] = total.astype(jnp.bfloat16)

            self.from_x[d] = [
                self.copy(self.has(y), self.x_out.at[y, lax.rem(self.x + e, SIZE_X)], self.x_in.at[e - 1, y], self.other_x(e))
                for e in (2, 1, 3)
            ]

    def x_to_y(self):
        self.from_y = []
        for d in Y_ORDER:
            y = lax.rem(self.y + d, SIZE_Y)

            @pl.when(self.has(y))
            def _(d=d, y=y):
                total = self.half[y, self.x]
                for copy in self.from_x[d]:
                    copy.wait_recv()
                for e in range(SIZE_X - 1):
                    total = total + self.x_in[e, y].astype(jnp.float32)
                if d:
                    self.y_out[d - 1] = total.astype(jnp.bfloat16)
                else:
                    self.half[y, self.x] = total

            if d:
                self.from_y.append(self.copy(self.has(y), self.y_out.at[d - 1], self.y_in.at[d - 1], self.other_y(d)))

    def y_to_z(self):
        @pl.when(self.mine)
        def _():
            total = self.half[self.y, self.x]
            for copy in self.from_y:
                copy.wait_recv()
            for d in range(SIZE_Y - 1):
                total = total + self.y_in[d].astype(jnp.float32)
            self.z_all[self.z] = total.astype(jnp.bfloat16)

        piece = self.z_all.at[self.z]
        self.from_z = [self.copy(self.mine, piece, piece, self.other_z(d)) for d in (4, 3, 5, 2, 6, 1, 7)]

    def spread_x(self, d):
        y = lax.rem(self.y + SIZE_Y - d, SIZE_Y)
        piece = self.done.at[self.core, self.x, y]
        for e in (2, 1, 3):
            self.gathered[e].append(self.copy(self.has(y), piece, piece, self.other_x(e)))

    def z_to_gather(self):
        @pl.when(self.mine)
        def _():
            for copy in self.from_z:
                copy.wait_recv()
            total = self.z_all[0].astype(jnp.float32)
            for other in range(1, SIZE_Z):
                total = total + self.z_all[other].astype(jnp.float32)
            self.done[self.core, self.x, self.y] = (total / self.scale).astype(jnp.bfloat16)

        piece = self.done.at[self.core, self.x, self.y]
        self.y_gathered = {d: self.copy(self.mine, piece, piece, self.other_y(d)) for d in (4, 3, 5, 2, 6, 1, 7)}
        self.gathered = {e: [] for e in range(1, SIZE_X)}
        self.spread_x(0)

    def gather_y(self):
        for d in GATHER_ORDER[1:]:
            pl.when(self.has(lax.rem(self.y + SIZE_Y - d, SIZE_Y)))(self.y_gathered[d].wait_recv)
            self.spread_x(d)
        self.spread_core(0)

    def spread_core(self, e):
        part = self.done.at[self.core, lax.rem(self.x + SIZE_X - e, SIZE_X), 0 : SIZE_Y - 1]
        self.copy(self.core >= 0, part, part, self.other_core())

    def gather_x(self):
        for e in (1, 3, 2):
            for d, copy in zip(GATHER_ORDER, self.gathered[e]):
                pl.when(self.has(lax.rem(self.y + SIZE_Y - d, SIZE_Y)))(copy.wait_recv)
            self.spread_core(e)

    def finish(self, out):
        for _, copy in self.sent[-SIZE_X:]:
            copy.wait_recv()
        for core in range(2):
            for part in range(SIZE_X):
                for y, slot, rows, lanes in self.places(core, part):
                    out[rows, lanes] = self.done[core, part, y, slot]
        for when, copy in self.sent:
            pl.when(when)(copy.wait_send)


def halo_peers():
    lon, lat = lax.axis_index("lon"), lax.axis_index("lat")
    count_lon, count_lat = lax.axis_size("lon"), lax.axis_size("lat")
    east, west = lax.rem(lon + 1, count_lon), lax.rem(lon + count_lon - 1, count_lon)
    south, north = lax.rem(lat + 1, count_lat), lax.rem(lat + count_lat - 1, count_lat)
    return {
        (row, column): {"lon": at_lon, "lat": at_lat}
        for row, at_lat in ((-1, north), (0, lat), (1, south))
        for column, at_lon in ((-1, west), (0, lon), (1, east))
        if (row, column) != (0, 0)
    }


class Halo:
    def __init__(self, own, west_in, east_in, west_out, east_out, send, recv, cuts):
        self.own, self.west_in, self.east_in = own, west_in, east_in
        self.west_out, self.east_out, self.send, self.recv = west_out, east_out, send, recv
        self.peers, self.rows, self.cuts, self.used = halo_peers(), own.shape[0] - 4, cuts, 0
        self.pairs, self.parts, self.top, self.bottom, self.sent = self.rows // 2, [], [], [], []

    def copy(self, src, dst, peer):
        index = self.used
        self.used += 1
        copy = pltpu.make_async_remote_copy(
            src_ref=src, dst_ref=dst, send_sem=self.send.at[index], recv_sem=self.recv.at[index],
            device_id=self.peers[peer], device_id_type=MESH)
        copy.start()
        self.sent.append(copy)
        return copy

    def left(self, part):
        for copy in self.parts[part]:
            copy.wait_send()
            self.sent = [other for other in self.sent if other is not copy]

    def drain(self):
        for copy in self.sent:
            copy.wait_send()

    def pack(self, first, values):
        pairs, channels = values.shape[0] // 2, values.shape[-1]
        split = values.reshape(pairs, 2, 16, channels)
        self.west_out[first : first + pairs] = split[:, :, :8].reshape(pairs, 16, channels).astype(jnp.bfloat16)
        self.east_out[first : first + pairs] = split[:, :, 8:].reshape(pairs, 16, channels).astype(jnp.bfloat16)

    def send_part(self, part):
        lo, hi = self.cuts[part], self.cuts[part + 1]
        self.parts.append([
            self.copy(self.east_out.at[lo:hi], self.west_in.at[lo + 1 : hi + 1], (0, 1)),
            self.copy(self.west_out.at[lo:hi], self.east_in.at[lo + 1 : hi + 1], (0, -1)),
        ])

    def send_north(self):
        rows, last = self.rows, self.pairs + 1
        self.bottom = [
            self.copy(self.own.at[2:4], self.own.at[rows + 2 : rows + 4], (-1, 0)),
            self.copy(self.east_out.at[0:1], self.west_in.at[last : last + 1], (-1, 1)),
            self.copy(self.west_out.at[0:1], self.east_in.at[last : last + 1], (-1, -1)),
        ]

    def send_south(self):
        rows, last = self.rows, self.pairs - 1
        self.top = [
            self.copy(self.own.at[rows : rows + 2], self.own.at[0:2], (1, 0)),
            self.copy(self.east_out.at[last : last + 1], self.west_in.at[0:1], (1, 1)),
            self.copy(self.west_out.at[last : last + 1], self.east_in.at[0:1], (1, -1)),
        ]

    def wait(self, copies):
        for copy in copies:
            copy.wait_recv()

    def window(self, first):
        channels = self.own.shape[-1]
        pair = first // 2
        return jnp.concatenate([
            self.own[first : first + 8].reshape(128, channels),
            self.west_in[pair : pair + 4].reshape(64, channels),
            self.east_in[pair : pair + 4].reshape(64, channels),
        ], axis=0)


def iota(shape, dim):
    return lax.broadcasted_iota(jnp.int32, shape, dim)


def lay_taps(filter_basis, half_widths, stage, taps):
    taps_lat, taps_lon, kernels, rows = filter_basis.shape
    allowed = jnp.abs(iota((taps_lon, rows), 0) - taps_lon // 2) <= half_widths[...].reshape(1, rows)
    stage[...] = jnp.zeros_like(stage)
    taps[...] = jnp.zeros_like(taps)
    for b in range(kernels):
        for s in range(taps_lat):
            values = jnp.where(allowed, filter_basis[s].astype(jnp.float32)[:, b], 0.0)
            stage[s * 32 : s * 32 + taps_lon, 0:rows] = values
        taps[b, 8 : 8 + stage.shape[1]] = stage[...].T


def base_rows(taps, b, first, rows, total_rows, backward):
    reach = 2
    near = taps[b, pl.ds(first, rows + 16)]
    lane = iota((rows, 256), 1)
    if not backward:
        source = iota((rows, 256), 0) + first + lax.div(lane, 32) - reach
        return jnp.where((source >= 0) & (source < total_rows), near[8 : 8 + rows], 0.0)
    chosen = jnp.zeros((rows, 256), jnp.float32)
    for s in range(5):
        start = 8 + reach - s
        chosen = jnp.where(lax.div(lane, 32) == s, near[start : start + rows], chosen)
    turned = (iota((256, 256), 0) + iota((256, 256), 1) == 144).astype(jnp.bfloat16)
    return jnp.dot(chosen.astype(jnp.bfloat16), turned, preferred_element_type=jnp.float32)


def lay_band(taps, base, moved, band, first, rows, total_rows, backward):
    kernels, blocks = taps.shape[0], rows // 4
    for b in range(kernels):
        base[b] = base_rows(taps, b, first, rows, total_rows, backward)

    def move(n, carry):
        for a in range(4):
            for b in range(kernels):
                row = jnp.broadcast_to(base[b, pl.ds(n * 4 + a, 1)], (16, 256))
                moved[a, n, b] = pltpu.roll(row, 0, 1, stride=1, stride_axis=0).astype(jnp.bfloat16)
        return carry

    lax.fori_loop(0, blocks, move, 0)
    place = iota((256, 256), 1)
    west, east = place - 128, place - 192
    own = lax.div(place, 16) * 32 + 8 + lax.rem(place, 16)
    side = jnp.where(place < 192, lax.div(west, 8) * 32 + lax.rem(west, 8), lax.div(east, 8) * 32 + 24 + lax.rem(east, 8))
    wanted = jnp.where(place < 128, own, side)
    for a in range(4):
        table = (iota((256, 256), 0) == wanted - 32 * a).astype(jnp.bfloat16)

        rows_in = moved[a].reshape(blocks * kernels * 16, 256)
        out = jnp.dot(rows_in, table, preferred_element_type=jnp.float32).astype(jnp.bfloat16)
        band[:, :, a] = out.reshape(blocks, kernels, 16, 256)


def gelu_slope(values):
    cdf = 0.5 * (1.0 + lax.erf(values * math.sqrt(0.5)))
    return cdf + values * (jnp.exp(values * values * -0.5) * (1.0 / math.sqrt(2.0 * math.pi)))


def apply_blocks(band, halo, flat, part, channels, blocks):
    for n in range(part * blocks, (part + 1) * blocks):
        out = jnp.dot(band[n].reshape(192, 256), halo.window(n * 4), preferred_element_type=jnp.float32).astype(jnp.bfloat16)
        for b in range(3):
            flat[n * 64 : (n + 1) * 64, b * channels : (b + 1) * channels] = out[b * 64 : (b + 1) * 64]


def block_kernel(
    scale, features_hbm, filter_hbm, half_widths, mixing_hbm, bias, cotangent_hbm, grad_hbm, mixing_out,
    own, west_in, east_in, west_out, east_out, send, recv,
    g_own, g_west_in, g_east_in, g_west_out, g_east_out, g_send, g_recv,
    mixing, cotangent, result, flat, local, stage, taps, base, moved, band, g_band, filter_basis, load_sem, store_sem, *sum_refs):
    rows, width, channels = cotangent.shape
    kernels, total_rows = filter_basis.shape[2:]
    parts, part_rows = 5, rows // 5
    blocks = part_rows // 4
    pairs = part_rows // 2
    loads = [
        pltpu.make_async_copy(features_hbm, own.at[2 : rows + 2], load_sem.at[0]),
        pltpu.make_async_copy(filter_hbm, filter_basis, load_sem.at[3]),
        pltpu.make_async_copy(mixing_hbm, mixing, load_sem.at[1]),
        pltpu.make_async_copy(cotangent_hbm, cotangent, load_sem.at[2]),
    ]
    for load in loads:
        load.start()
    peers = list(halo_peers().values()) + sum_peers()
    greet(peers)
    work = SumOverAll(mixing.shape[0] // (2 * SIZE_X), channels, sum_refs, scale)
    cuts = [0] + [pairs * part + 1 for part in range(1, parts)] + [rows // 2]
    halo = Halo(own, west_in, east_in, west_out, east_out, send, recv, cuts)
    g_halo = Halo(g_own, g_west_in, g_east_in, g_west_out, g_east_out, g_send, g_recv, [pairs * part for part in range(parts + 1)])
    loads[0].wait()
    for part in range(parts):
        lo, hi = cuts[part], cuts[part + 1]
        halo.pack(lo, own[2 + 2 * lo : 2 + 2 * hi].astype(jnp.float32))
    work.clear()
    await_greetings(len(peers))
    halo.send_north()
    halo.send_south()
    halo.send_part(0)
    halo.send_part(1)

    first = pl.multiple_of(lax.axis_index("lat") * rows, 8)
    loads[1].wait()
    lay_taps(filter_basis, half_widths, stage, taps)
    lay_band(taps, base, moved, band, first, rows, total_rows, False)
    for part in (0, 1):
        halo.left(part)
        halo.send_part(part + 2)
    loads[2].wait()
    loads[3].wait()
    halo.wait(halo.top)
    cells = part_rows * width
    for part in range(parts):
        halo.wait(halo.parts[part])
        if part == 1:
            halo.left(2)
            halo.send_part(4)
        if part == parts - 1:
            halo.wait(halo.bottom)
        apply_blocks(band, halo, flat, part, channels, blocks)
        here = flat[part * cells : (part + 1) * cells]
        pre = jnp.dot(here, mixing[...], preferred_element_type=jnp.float32) + bias[...].reshape(1, channels)
        at = part * part_rows
        cot = cotangent[at : at + part_rows].reshape(cells, channels).astype(jnp.float32)
        grad = cot * gelu_slope(pre)
        grad_rows = grad.reshape(part_rows, width, channels)
        grad = grad.astype(jnp.bfloat16)
        g_own[2 + at : 2 + at + part_rows] = grad.reshape(part_rows, width, channels)
        g_halo.pack(at // 2, grad_rows)
        g_halo.send_part(part)
        if part == 0:
            g_halo.send_north()
        if part == parts - 1:
            g_halo.send_south()
        outer = lax.dot_general(here, grad, (((0,), (0,)), ((), ())), preferred_element_type=jnp.float32)
        if part == 0:
            local[...] = outer
        elif part < parts - 1:
            local[...] += outer
        else:
            work.lay(outer, local)

    work.start_core()
    work.core_to_x()
    lay_band(taps, base, moved, g_band, first, rows, total_rows, True)
    work.x_to_y()
    work.y_to_z()
    steps = {2: work.z_to_gather, 3: work.gather_y}
    stores = []
    g_halo.wait(g_halo.top)
    g_halo.wait(g_halo.parts[0])
    for part in range(parts):
        if part in steps:
            steps[part]()
        if part < parts - 1:
            g_halo.wait(g_halo.parts[part + 1])
        else:
            g_halo.wait(g_halo.bottom)
        apply_blocks(g_band, g_halo, flat, part, channels, blocks)
        here = flat[part * cells : (part + 1) * cells]
        at = part * part_rows
        branch = cotangent[at : at + part_rows].reshape(cells, channels).astype(jnp.float32)
        for b in range(kernels):
            mix = mixing[b * channels : (b + 1) * channels]
            branch = branch + lax.dot_general(
                here[:, b * channels : (b + 1) * channels], mix, (((1,), (1,)), ((), ())), preferred_element_type=jnp.float32)
        result[at : at + part_rows] = branch.astype(jnp.bfloat16).reshape(part_rows, width, channels)
        stores.append(pltpu.make_async_copy(
            result.at[at : at + part_rows], grad_hbm.at[at : at + part_rows], store_sem.at[part]))
        stores[-1].start()
    work.gather_x()
    work.finish(mixing_out)
    for store in stores:
        store.wait()
    halo.drain()
    g_halo.drain()


def halo_buffers(rows, channels, parts):
    side = pltpu.VMEM((rows // 2 + 2, 16, channels), jnp.bfloat16)
    out = pltpu.VMEM((rows // 2, 16, channels), jnp.bfloat16)
    copies = 2 * parts + 6
    return [
        pltpu.VMEM((rows + 4, 16, channels), jnp.bfloat16), side, side, out, out,
        pltpu.SemaphoreType.DMA((copies,)), pltpu.SemaphoreType.DMA((copies,)),
    ]


def per_device(features, filter_basis, half_widths, mixing, channel_bias, cotangent):
    rows, width, channels = features.shape
    kernels, taps_lat, taps_lon, total_rows = filter_basis.shape
    cells = rows * width
    cell_count = cells * lax.axis_size("lat") * lax.axis_size("lon")
    blocks = rows // 4
    lanes = -(-total_rows // 128) * 128
    anywhere, vmem = pl.BlockSpec(memory_space=pltpu.HBM), pl.BlockSpec(memory_space=pltpu.VMEM)
    band = pltpu.VMEM((blocks, kernels, 4, 16, 256), jnp.bfloat16)
    return pl.pallas_call(
        lambda *refs: block_kernel(math.sqrt(cell_count), *refs),
        out_shape=(
            jax.ShapeDtypeStruct((rows, width, channels), jnp.bfloat16),
            jax.ShapeDtypeStruct((kernels * channels, channels), jnp.bfloat16),
        ),
        in_specs=[anywhere, anywhere, vmem, anywhere, vmem, anywhere],
        out_specs=(anywhere, vmem),
        scratch_shapes=[
            *halo_buffers(rows, channels, 5),
            *halo_buffers(rows, channels, 5),
            pltpu.VMEM((kernels * channels, channels), jnp.bfloat16),
            pltpu.VMEM((rows, width, channels), jnp.bfloat16),
            pltpu.VMEM((rows, width, channels), jnp.bfloat16),
            pltpu.VMEM((cells, kernels * channels), jnp.bfloat16),
            pltpu.VMEM((kernels * channels, channels), jnp.float32),
            pltpu.VMEM((256, lanes), jnp.float32),
            pltpu.VMEM((kernels, lanes + 16, 256), jnp.float32),
            pltpu.VMEM((kernels, rows, 256), jnp.float32),
            pltpu.VMEM((4, blocks, kernels, 16, 256), jnp.bfloat16),
            band,
            band,
            pltpu.VMEM((taps_lat, taps_lon, kernels, total_rows), jnp.bfloat16),
            pltpu.SemaphoreType.DMA((4,)),
            pltpu.SemaphoreType.DMA((5,)),
            *sum_buffers(),
        ],
        compiler_params=pltpu.CompilerParams(
            collective_id=0, has_side_effects=True, vmem_limit_bytes=56 * 1024 * 1024),
    )(features, filter_basis.transpose(1, 2, 0, 3), half_widths, mixing, channel_bias, cotangent)


def solution(mesh):
    return jax.shard_map(
        per_device,
        mesh=mesh,
        in_specs=(P("lat", "lon", None), P(), P(), P(), P(), P("lat", "lon", None)),
        out_specs=(P("lat", "lon", None), P()),
        check_vma=False,
    )
```

```python
import math

import jax
import jax.numpy as jnp
from jax import lax
from jax.experimental import pallas as pl
from jax.experimental.pallas import tpu as pltpu
from jax.sharding import PartitionSpec as P

MESH = pl.DeviceIdType.MESH
SIZE_X_LO, SIZE_Z, SIZE_Y = 2, 8, 8
SIZE_X = 4


def position():
    lon, lat = lax.axis_index("lon"), lax.axis_index("lat")
    x = lax.div(lat, 2) * SIZE_X_LO + lax.div(lon, SIZE_Z * SIZE_Y)
    z = lax.rem(lax.div(lon, SIZE_Y), SIZE_Z)
    return x, z, lax.rem(lon, SIZE_Y), lax.rem(lat, 2)


def device(x, z, y, core):
    lon = (lax.rem(x, SIZE_X_LO) * SIZE_Z + z) * SIZE_Y + y
    return {"lon": lon, "lat": lax.div(x, SIZE_X_LO) * 2 + core}


def sum_peers():
    x, z, y, core = position()
    peers = [device(x, z, y, 1 - core)]
    peers += [device(lax.rem(x + d, SIZE_X), z, y, core) for d in range(1, SIZE_X)]
    peers += [device(x, lax.rem(z + d, SIZE_Z), y, core) for d in range(1, SIZE_Z)]
    peers += [device(x, z, lax.rem(y + d, SIZE_Y), core) for d in range(1, SIZE_Y)]
    return peers


def greet(peers):
    barrier = pltpu.get_barrier_semaphore()
    for peer in peers:
        pl.semaphore_signal(barrier, inc=1, device_id=peer, device_id_type=MESH)


def await_greetings(count):
    pl.semaphore_wait(pltpu.get_barrier_semaphore(), count)


SHARE = 4
Y_ORDER = (4, 3, 5, 2, 6, 1, 7, 0)
GATHER_ORDER = (0, 1, 7, 2, 6, 3, 5, 4)


def tile_count(part_rows, channels):
    tiles = (part_rows // 16) * (channels // 128)
    assert (SIZE_Y - 1) * SHARE <= tiles + 1 <= SIZE_Y * SHARE
    return tiles


def sum_buffers():
    pieces = (SIZE_Y, SIZE_X, SHARE, 16, 128)
    copies = SIZE_Y + 2 * SIZE_Y * (SIZE_X - 1) + 2 * (SIZE_Y - 1) + SIZE_Z - 1 + SIZE_X
    return [
        pltpu.VMEM((2, *pieces), jnp.float32),
        pltpu.VMEM(pieces, jnp.float32),
        pltpu.VMEM(pieces, jnp.bfloat16),
        pltpu.VMEM((SIZE_X - 1, SIZE_Y, SHARE, 16, 128), jnp.bfloat16),
        pltpu.VMEM((SIZE_Y - 1, SHARE, 16, 128), jnp.bfloat16),
        pltpu.VMEM((SIZE_Y - 1, SHARE, 16, 128), jnp.bfloat16),
        pltpu.VMEM((SIZE_Z, SHARE, 16, 128), jnp.bfloat16),
        pltpu.VMEM((2, SIZE_X, SIZE_Y, SHARE, 16, 128), jnp.bfloat16),
        pltpu.SemaphoreType.DMA((copies,)),
        pltpu.SemaphoreType.DMA((copies,)),
    ]


class SumOverAll:
    def __init__(self, rows, channels, buffers, scale):
        (self.local, self.half, self.x_out, self.x_in, self.y_out, self.y_in, self.z_all, self.done, self.send, self.recv) = buffers
        self.rows, self.lanes, self.tiles, self.scale = rows, channels // 128, tile_count(rows, channels), scale
        self.x, self.z, self.y, self.core = position()
        self.used, self.sent = 0, []
        self.mine = self.has(self.y)

    def has(self, y):
        return y < SIZE_Y - 1

    def copy(self, when, src, dst, peer):
        index = self.used
        self.used += 1
        copy = pltpu.make_async_remote_copy(
            src_ref=src, dst_ref=dst, send_sem=self.send.at[index], recv_sem=self.recv.at[index],
            device_id=peer, device_id_type=MESH)
        pl.when(when)(copy.start)
        self.sent.append((when, copy))
        return copy

    def other_core(self):
        return device(self.x, self.z, self.y, 1 - self.core)

    def other_x(self, d):
        return device(lax.rem(self.x + d, SIZE_X), self.z, self.y, self.core)

    def other_y(self, d):
        return device(self.x, self.z, lax.rem(self.y + d, SIZE_Y), self.core)

    def other_z(self, d):
        return device(self.x, lax.rem(self.z + d, SIZE_Z), self.y, self.core)

    def places(self, core, part):
        for t in range(self.tiles):
            row = (core * SIZE_X + part) * self.rows + t // self.lanes * 16
            lane = t % self.lanes * 128
            yield t // SHARE, t % SHARE, slice(row, row + 16), slice(lane, lane + 128)

    def clear(self):
        self.local[:, SIZE_Y - 2 :] = jnp.zeros_like(self.local[:, SIZE_Y - 2 :])

    def lay(self, values, more):
        for core in range(2):
            for part in range(SIZE_X):
                for y, slot, rows, lanes in self.places(core, part):
                    self.local[core, y, part, slot] = values[rows, lanes] + more[rows, lanes]

    def start_core(self):
        self.from_core = {}
        for d in Y_ORDER:
            y = lax.rem(self.y + d, SIZE_Y)
            self.from_core[d] = self.copy(self.has(y), self.local.at[1 - self.core, y], self.half.at[y], self.other_core())

    def core_to_x(self):
        self.from_x = {}
        for d in Y_ORDER:
            y = lax.rem(self.y + d, SIZE_Y)

            @pl.when(self.has(y))
            def _(d=d, y=y):
                self.from_core[d].wait_recv()
                total = self.half[y] + self.local[self.core, y]
                self.half[y] = total
                self.x_out[y] = total.astype(jnp.bfloat16)

            self.from_x[d] = [
                self.copy(self.has(y), self.x_out.at[y, lax.rem(self.x + e, SIZE_X)], self.x_in.at[e - 1, y], self.other_x(e))
                for e in (2, 1, 3)
            ]

    def x_to_y(self):
        self.from_y = []
        for d in Y_ORDER:
            y = lax.rem(self.y + d, SIZE_Y)

            @pl.when(self.has(y))
            def _(d=d, y=y):
                total = self.half[y, self.x]
                for copy in self.from_x[d]:
                    copy.wait_recv()
                for e in range(SIZE_X - 1):
                    total = total + self.x_in[e, y].astype(jnp.float32)
                if d:
                    self.y_out[d - 1] = total.astype(jnp.bfloat16)
                else:
                    self.half[y, self.x] = total

            if d:
                self.from_y.append(self.copy(self.has(y), self.y_out.at[d - 1], self.y_in.at[d - 1], self.other_y(d)))

    def y_to_z(self):
        @pl.when(self.mine)
        def _():
            total = self.half[self.y, self.x]
            for copy in self.from_y:
                copy.wait_recv()
            for d in range(SIZE_Y - 1):
                total = total + self.y_in[d].astype(jnp.float32)
            self.z_all[self.z] = total.astype(jnp.bfloat16)

        piece = self.z_all.at[self.z]
        self.from_z = [self.copy(self.mine, piece, piece, self.other_z(d)) for d in (4, 3, 5, 2, 6, 1, 7)]

    def spread_x(self, d):
        y = lax.rem(self.y + SIZE_Y - d, SIZE_Y)
        piece = self.done.at[self.core, self.x, y]
        for e in (2, 1, 3):
            self.gathered[e].append(self.copy(self.has(y), piece, piece, self.other_x(e)))

    def z_to_gather(self):
        @pl.when(self.mine)
        def _():
            for copy in self.from_z:
                copy.wait_recv()
            total = self.z_all[0].astype(jnp.float32)
            for other in range(1, SIZE_Z):
                total = total + self.z_all[other].astype(jnp.float32)
            self.done[self.core, self.x, self.y] = (total / self.scale).astype(jnp.bfloat16)

        piece = self.done.at[self.core, self.x, self.y]
        self.y_gathered = {d: self.copy(self.mine, piece, piece, self.other_y(d)) for d in (4, 3, 5, 2, 6, 1, 7)}
        self.gathered = {e: [] for e in range(1, SIZE_X)}
        self.spread_x(0)

    def gather_y(self):
        for d in GATHER_ORDER[1:]:
            pl.when(self.has(lax.rem(self.y + SIZE_Y - d, SIZE_Y)))(self.y_gathered[d].wait_recv)
            self.spread_x(d)
        self.spread_core(0)

    def spread_core(self, e):
        part = self.done.at[self.core, lax.rem(self.x + SIZE_X - e, SIZE_X), 0 : SIZE_Y - 1]
        self.copy(self.core >= 0, part, part, self.other_core())

    def gather_x(self):
        for e in (1, 3, 2):
            for d, copy in zip(GATHER_ORDER, self.gathered[e]):
                pl.when(self.has(lax.rem(self.y + SIZE_Y - d, SIZE_Y)))(copy.wait_recv)
            self.spread_core(e)

    def finish(self, out):
        for _, copy in self.sent[-SIZE_X:]:
            copy.wait_recv()
        for core in range(2):
            for part in range(SIZE_X):
                for y, slot, rows, lanes in self.places(core, part):
                    out[rows, lanes] = self.done[core, part, y, slot]
        for when, copy in self.sent:
            pl.when(when)(copy.wait_send)


def halo_peers():
    lon, lat = lax.axis_index("lon"), lax.axis_index("lat")
    count_lon, count_lat = lax.axis_size("lon"), lax.axis_size("lat")
    east, west = lax.rem(lon + 1, count_lon), lax.rem(lon + count_lon - 1, count_lon)
    south, north = lax.rem(lat + 1, count_lat), lax.rem(lat + count_lat - 1, count_lat)
    return {
        (row, column): {"lon": at_lon, "lat": at_lat}
        for row, at_lat in ((-1, north), (0, lat), (1, south))
        for column, at_lon in ((-1, west), (0, lon), (1, east))
        if (row, column) != (0, 0)
    }


class Halo:
    def __init__(self, own, west_in, east_in, west_out, east_out, send, recv, cuts):
        self.own, self.west_in, self.east_in = own, west_in, east_in
        self.west_out, self.east_out, self.send, self.recv = west_out, east_out, send, recv
        self.peers, self.rows, self.cuts, self.used = halo_peers(), own.shape[0] - 4, cuts, 0
        self.pairs, self.parts, self.top, self.bottom, self.sent = self.rows // 2, [], [], [], []

    def copy(self, src, dst, peer):
        index = self.used
        self.used += 1
        copy = pltpu.make_async_remote_copy(
            src_ref=src, dst_ref=dst, send_sem=self.send.at[index], recv_sem=self.recv.at[index],
            device_id=self.peers[peer], device_id_type=MESH)
        copy.start()
        self.sent.append(copy)
        return copy

    def left(self, part):
        for copy in self.parts[part]:
            copy.wait_send()
            self.sent = [other for other in self.sent if other is not copy]

    def drain(self):
        for copy in self.sent:
            copy.wait_send()

    def pack(self, first, values):
        pairs, channels = values.shape[0] // 2, values.shape[-1]
        split = values.reshape(pairs, 2, 16, channels)
        self.west_out[first : first + pairs] = split[:, :, :8].reshape(pairs, 16, channels).astype(jnp.bfloat16)
        self.east_out[first : first + pairs] = split[:, :, 8:].reshape(pairs, 16, channels).astype(jnp.bfloat16)

    def send_part(self, part):
        lo, hi = self.cuts[part], self.cuts[part + 1]
        self.parts.append([
            self.copy(self.east_out.at[lo:hi], self.west_in.at[lo + 1 : hi + 1], (0, 1)),
            self.copy(self.west_out.at[lo:hi], self.east_in.at[lo + 1 : hi + 1], (0, -1)),
        ])

    def send_north(self):
        rows, last = self.rows, self.pairs + 1
        self.bottom = [
            self.copy(self.own.at[2:4], self.own.at[rows + 2 : rows + 4], (-1, 0)),
            self.copy(self.east_out.at[0:1], self.west_in.at[last : last + 1], (-1, 1)),
            self.copy(self.west_out.at[0:1], self.east_in.at[last : last + 1], (-1, -1)),
        ]

    def send_south(self):
        rows, last = self.rows, self.pairs - 1
        self.top = [
            self.copy(self.own.at[rows : rows + 2], self.own.at[0:2], (1, 0)),
            self.copy(self.east_out.at[last : last + 1], self.west_in.at[0:1], (1, 1)),
            self.copy(self.west_out.at[last : last + 1], self.east_in.at[0:1], (1, -1)),
        ]

    def wait(self, copies):
        for copy in copies:
            copy.wait_recv()

    def window(self, first):
        channels = self.own.shape[-1]
        pair = first // 2
        return jnp.concatenate([
            self.own[first : first + 8].reshape(128, channels),
            self.west_in[pair : pair + 4].reshape(64, channels),
            self.east_in[pair : pair + 4].reshape(64, channels),
        ], axis=0)


def iota(shape, dim):
    return lax.broadcasted_iota(jnp.int32, shape, dim)


def lay_taps(filter_basis, half_widths, stage, taps):
    taps_lat, taps_lon, kernels, rows = filter_basis.shape
    allowed = jnp.abs(iota((taps_lon, rows), 0) - taps_lon // 2) <= half_widths[...].reshape(1, rows)
    stage[...] = jnp.zeros_like(stage)
    taps[...] = jnp.zeros_like(taps)
    for b in range(kernels):
        for s in range(taps_lat):
            values = jnp.where(allowed, filter_basis[s].astype(jnp.float32)[:, b], 0.0)
            stage[s * 32 : s * 32 + taps_lon, 0:rows] = values
        taps[b, 8 : 8 + stage.shape[1]] = stage[...].T


def base_rows(taps, b, first, rows, total_rows, backward):
    reach = 2
    near = taps[b, pl.ds(first, rows + 16)]
    lane = iota((rows, 256), 1)
    if not backward:
        source = iota((rows, 256), 0) + first + lax.div(lane, 32) - reach
        return jnp.where((source >= 0) & (source < total_rows), near[8 : 8 + rows], 0.0)
    chosen = jnp.zeros((rows, 256), jnp.float32)
    for s in range(5):
        start = 8 + reach - s
        chosen = jnp.where(lax.div(lane, 32) == s, near[start : start + rows], chosen)
    turned = (iota((256, 256), 0) + iota((256, 256), 1) == 144).astype(jnp.bfloat16)
    return jnp.dot(chosen.astype(jnp.bfloat16), turned, preferred_element_type=jnp.float32)


def lay_band(taps, base, moved, band, first, rows, total_rows, backward):
    kernels, blocks = taps.shape[0], rows // 4
    for b in range(kernels):
        base[b] = base_rows(taps, b, first, rows, total_rows, backward)

    def move(n, carry):
        for a in range(4):
            for b in range(kernels):
                row = jnp.broadcast_to(base[b, pl.ds(n * 4 + a, 1)], (16, 256))
                moved[a, n, b] = pltpu.roll(row, 0, 1, stride=1, stride_axis=0).astype(jnp.bfloat16)
        return carry

    lax.fori_loop(0, blocks, move, 0)
    place = iota((256, 256), 1)
    west, east = place - 128, place - 192
    own = lax.div(place, 16) * 32 + 8 + lax.rem(place, 16)
    side = jnp.where(place < 192, lax.div(west, 8) * 32 + lax.rem(west, 8), lax.div(east, 8) * 32 + 24 + lax.rem(east, 8))
    wanted = jnp.where(place < 128, own, side)
    for a in range(4):
        table = (iota((256, 256), 0) == wanted - 32 * a).astype(jnp.bfloat16)

        rows_in = moved[a].reshape(blocks * kernels * 16, 256)
        out = jnp.dot(rows_in, table, preferred_element_type=jnp.float32).astype(jnp.bfloat16)
        band[:, :, a] = out.reshape(blocks, kernels, 16, 256)


def gelu_slope(values):
    cdf = 0.5 * (1.0 + lax.erf(values * math.sqrt(0.5)))
    return cdf + values * (jnp.exp(values * values * -0.5) * (1.0 / math.sqrt(2.0 * math.pi)))


def apply_blocks(band, halo, flat, part, channels, blocks):
    for n in range(part * blocks, (part + 1) * blocks):
        out = jnp.dot(band[n].reshape(192, 256), halo.window(n * 4), preferred_element_type=jnp.float32).astype(jnp.bfloat16)
        for b in range(3):
            flat[n * 64 : (n + 1) * 64, b * channels : (b + 1) * channels] = out[b * 64 : (b + 1) * 64]


def block_kernel(
    scale, features_hbm, filter_hbm, half_widths, mixing_hbm, bias, cotangent_hbm, grad_hbm, mixing_out,
    own, west_in, east_in, west_out, east_out, send, recv,
    g_own, g_west_in, g_east_in, g_west_out, g_east_out, g_send, g_recv,
    mixing, cotangent, result, flat, local, stage, taps, base, moved, band, g_band, filter_basis, load_sem, store_sem, *sum_refs):
    rows, width, channels = cotangent.shape
    kernels, total_rows = filter_basis.shape[2:]
    parts, part_rows = 5, rows // 5
    blocks = part_rows // 4
    pairs = part_rows // 2
    loads = [
        pltpu.make_async_copy(features_hbm, own.at[2 : rows + 2], load_sem.at[0]),
        pltpu.make_async_copy(filter_hbm, filter_basis, load_sem.at[3]),
        pltpu.make_async_copy(mixing_hbm, mixing, load_sem.at[1]),
        pltpu.make_async_copy(cotangent_hbm, cotangent, load_sem.at[2]),
    ]
    loads[0].start()
    peers = list(halo_peers().values()) + sum_peers()
    greet(peers)
    work = SumOverAll(mixing.shape[0] // (2 * SIZE_X), channels, sum_refs, scale)
    cuts = [0] + [pairs * part + 1 for part in range(1, parts)] + [rows // 2]
    halo = Halo(own, west_in, east_in, west_out, east_out, send, recv, cuts)
    g_halo = Halo(g_own, g_west_in, g_east_in, g_west_out, g_east_out, g_send, g_recv, [pairs * part for part in range(parts + 1)])
    loads[0].wait()
    for load in loads[1:]:
        load.start()
    for part in range(parts):
        lo, hi = cuts[part], cuts[part + 1]
        halo.pack(lo, own[2 + 2 * lo : 2 + 2 * hi].astype(jnp.float32))
    work.clear()
    await_greetings(len(peers))
    halo.send_north()
    halo.send_south()
    halo.send_part(0)
    halo.send_part(1)

    first = pl.multiple_of(lax.axis_index("lat") * rows, 8)
    loads[1].wait()
    lay_taps(filter_basis, half_widths, stage, taps)
    lay_band(taps, base, moved, band, first, rows, total_rows, False)
    for part in (0, 1):
        halo.left(part)
        halo.send_part(part + 2)
    loads[2].wait()
    loads[3].wait()
    halo.wait(halo.top)
    cells = part_rows * width
    for part in range(parts):
        halo.wait(halo.parts[part])
        if part == 0:
            halo.send_part(4)
        if part == parts - 1:
            halo.wait(halo.bottom)
        apply_blocks(band, halo, flat, part, channels, blocks)
        here = flat[part * cells : (part + 1) * cells]
        pre = jnp.dot(here, mixing[...], preferred_element_type=jnp.float32) + bias[...].reshape(1, channels)
        at = part * part_rows
        cot = cotangent[at : at + part_rows].reshape(cells, channels).astype(jnp.float32)
        grad = cot * gelu_slope(pre)
        grad_rows = grad.reshape(part_rows, width, channels)
        grad = grad.astype(jnp.bfloat16)
        g_own[2 + at : 2 + at + part_rows] = grad.reshape(part_rows, width, channels)
        g_halo.pack(at // 2, grad_rows)
        g_halo.send_part(part)
        if part == 0:
            g_halo.send_north()
        if part == parts - 1:
            g_halo.send_south()
        outer = lax.dot_general(here, grad, (((0,), (0,)), ((), ())), preferred_element_type=jnp.float32)
        if part == 0:
            local[...] = outer
        elif part < parts - 1:
            local[...] += outer
        else:
            work.lay(outer, local)

    work.start_core()
    work.core_to_x()
    lay_band(taps, base, moved, g_band, first, rows, total_rows, True)
    work.x_to_y()
    work.y_to_z()
    steps = {2: work.z_to_gather, 3: work.gather_y}
    stores = []
    g_halo.wait(g_halo.top)
    g_halo.wait(g_halo.parts[0])
    for part in range(parts):
        if part in steps:
            steps[part]()
        if part < parts - 1:
            g_halo.wait(g_halo.parts[part + 1])
        else:
            g_halo.wait(g_halo.bottom)
        apply_blocks(g_band, g_halo, flat, part, channels, blocks)
        here = flat[part * cells : (part + 1) * cells]
        at = part * part_rows
        branch = cotangent[at : at + part_rows].reshape(cells, channels).astype(jnp.float32)
        for b in range(kernels):
            mix = mixing[b * channels : (b + 1) * channels]
            branch = branch + lax.dot_general(
                here[:, b * channels : (b + 1) * channels], mix, (((1,), (1,)), ((), ())), preferred_element_type=jnp.float32)
        result[at : at + part_rows] = branch.astype(jnp.bfloat16).reshape(part_rows, width, channels)
        stores.append(pltpu.make_async_copy(
            result.at[at : at + part_rows], grad_hbm.at[at : at + part_rows], store_sem.at[part]))
        stores[-1].start()
    work.gather_x()
    work.finish(mixing_out)
    for store in stores:
        store.wait()
    halo.drain()
    g_halo.drain()


def halo_buffers(rows, channels, parts):
    side = pltpu.VMEM((rows // 2 + 2, 16, channels), jnp.bfloat16)
    out = pltpu.VMEM((rows // 2, 16, channels), jnp.bfloat16)
    copies = 2 * parts + 6
    return [
        pltpu.VMEM((rows + 4, 16, channels), jnp.bfloat16), side, side, out, out,
        pltpu.SemaphoreType.DMA((copies,)), pltpu.SemaphoreType.DMA((copies,)),
    ]


def per_device(features, filter_basis, half_widths, mixing, channel_bias, cotangent):
    rows, width, channels = features.shape
    kernels, taps_lat, taps_lon, total_rows = filter_basis.shape
    cells = rows * width
    cell_count = cells * lax.axis_size("lat") * lax.axis_size("lon")
    blocks = rows // 4
    lanes = -(-total_rows // 128) * 128
    anywhere, vmem = pl.BlockSpec(memory_space=pltpu.HBM), pl.BlockSpec(memory_space=pltpu.VMEM)
    band = pltpu.VMEM((blocks, kernels, 4, 16, 256), jnp.bfloat16)
    return pl.pallas_call(
        lambda *refs: block_kernel(math.sqrt(cell_count), *refs),
        out_shape=(
            jax.ShapeDtypeStruct((rows, width, channels), jnp.bfloat16),
            jax.ShapeDtypeStruct((kernels * channels, channels), jnp.bfloat16),
        ),
        in_specs=[anywhere, anywhere, vmem, anywhere, vmem, anywhere],
        out_specs=(anywhere, vmem),
        scratch_shapes=[
            *halo_buffers(rows, channels, 5),
            *halo_buffers(rows, channels, 5),
            pltpu.VMEM((kernels * channels, channels), jnp.bfloat16),
            pltpu.VMEM((rows, width, channels), jnp.bfloat16),
            pltpu.VMEM((rows, width, channels), jnp.bfloat16),
            pltpu.VMEM((cells, kernels * channels), jnp.bfloat16),
            pltpu.VMEM((kernels * channels, channels), jnp.float32),
            pltpu.VMEM((256, lanes), jnp.float32),
            pltpu.VMEM((kernels, lanes + 16, 256), jnp.float32),
            pltpu.VMEM((kernels, rows, 256), jnp.float32),
            pltpu.VMEM((4, blocks, kernels, 16, 256), jnp.bfloat16),
            band,
            band,
            pltpu.VMEM((taps_lat, taps_lon, kernels, total_rows), jnp.bfloat16),
            pltpu.SemaphoreType.DMA((4,)),
            pltpu.SemaphoreType.DMA((5,)),
            *sum_buffers(),
        ],
        compiler_params=pltpu.CompilerParams(
            collective_id=0, has_side_effects=True, vmem_limit_bytes=56 * 1024 * 1024),
    )(features, filter_basis.transpose(1, 2, 0, 3), half_widths, mixing, channel_bias, cotangent)


def solution(mesh):
    return jax.shard_map(
        per_device,
        mesh=mesh,
        in_specs=(P("lat", "lon", None), P(), P(), P(), P(), P("lat", "lon", None)),
        out_specs=(P("lat", "lon", None), P()),
        check_vma=False,
    )
```
